128 devices in a mesh: fsdp: 16 (over x_lo, z, core), tp: 8 (over x_hi, y).
Axes of the slice: x: 4 (x_hi: 2, x_lo: 2; x = x_hi * 2 + x_lo), y: 4, z: 4, core: 2. Of those that a mesh axis runs over, the one named last changes fastest.
Arguments:
- inputs: bfloat16 [2, 128, 8192], P(None, 'tp'), may hold values from -6 to 6
- w_xz: bfloat16 [8192, 128, 128], P('fsdp', 'tp'), may hold values from -0.0625 to 0.0625
- w_dt: bfloat16 [8192, 128], P('fsdp', 'tp'), may hold values from -0.0625 to 0.0625
- w_bc: bfloat16 [8192, 2048], P('fsdp', 'tp'), may hold values from -0.0625 to 0.0625
- w_out: bfloat16 [128, 64, 8192], P('tp', None, 'fsdp'), may hold values from -0.0625 to 0.0625
- head_map: int32 [16], replicated, may hold values from 0 to 15, each once
- a_log: float32 [128], replicated, may hold values from 0 to 2.77
- dt_bias: float32 [128], replicated, may hold values from -4 to -1
- skip_coef: float32 [128], replicated, may hold values from 0.5 to 2.5
- conv_x: float32 [5, 8192], replicated, may hold values from -3 to 3
- conv_bc: float32 [5, 2048], replicated, may hold values from -3 to 3
- norm_gain: float32 [8192], replicated, may hold values from 0.25 to 1.75
- ssm_state: float32 [128, 128, 64, 256], P('tp', 'fsdp'), may hold values from -26 to 26, as said below
- conv_x_state: float32 [128, 3, 8192], P('tp', None, 'fsdp'), may hold values from -6 to 6
- conv_bc_state: float32 [128, 3, 2048], P('tp'), may hold values from -6 to 6
Outputs:
- mixed: bfloat16 [2, 128, 8192], P(None, 'tp', 'fsdp')
- ssm_state_out: float32 [128, 128, 64, 256], P('tp', 'fsdp')
- conv_x_state_out: float32 [128, 3, 8192], P('tp', None, 'fsdp')
- conv_bc_state_out: float32 [128, 3, 2048], P('tp')
The draws below stay inside these ranges and needn't reach their ends.
Inputs may be any that keep to these rules, and one draw needn't show every extreme that they name: `ssm_state`: the rollout's recurrent states.
All inputs are finite; a program needn't handle non-finite values.
Results may differ from the reference program's by a relative error of at most 0.0052.
Values may be sent and summed in bfloat16 or wider, within the bound.
No kernel may reach another device: no remote copies, remote signals or barrier semaphores. Data moves between devices by JAX's collectives and lax.ppermute only.
A program may use at most 192 MiB of HBM per device.

```python
import jax
import jax.numpy as jnp
from jax import lax

D = 8192
HEADS = 128
HEAD_DIM = 64
STATE = 256
GROUPS = 4
KERNEL = 4
ROWS = 16
STEPS = 2
ROWS_TOT = 128
INNER = 8192
BC_WIDTH = 2048
SLICES = 16
HEAD_SLOTS = 8
N_TP = 8


def draw_ssm_state(key, part):
    key = jax.random.fold_in(key, 11)
    base_key, row_key, slot_key = jax.random.split(key, 3)
    full_shape = (ROWS_TOT, HEADS, HEAD_DIM, STATE)
    base_draw = jax.random.normal(base_key, full_shape, jnp.float32)
    base_draw = jnp.clip(base_draw, -6.0, 6.0)
    row_scale = 10.0 ** (jax.random.uniform(row_key, (ROWS_TOT, 1, 1, 1), jnp.float32) - 1.0)
    slot_pos = jnp.arange(HEADS, dtype=jnp.float32) / HEADS
    slot_scale = 10.0 ** (slot_pos - 0.5) * jnp.exp(jax.random.uniform(slot_key, (HEADS,), jnp.float32, -0.3, 0.3))
    return base_draw * row_scale * slot_scale[None, :, None, None]


def levels(rng, dims, pieces, smallest, high):
    def one(position, parts):
        draws = jax.random.uniform(jax.random.fold_in(jax.random.fold_in(rng, 6), position), (parts,), jnp.float32, smallest / len(pieces), high / len(pieces))
        return jnp.repeat(jnp.exp(draws), dims[position] // parts).reshape((-1,) + (1,) * (len(dims) - position - 1))

    gain = one(*pieces[0])
    for cut in pieces[1:]:
        gain = gain * one(*cut)
    return gain


def normal_values(stream_key, shape, deviation, most, pieces=(), kind=jnp.bfloat16):
    result = jax.random.normal(stream_key, shape, jnp.float32) * deviation
    if len(pieces) > 0:
        result = levels(stream_key, shape, pieces, -0.22, 0.18) * result
    return jnp.clip(result, min=-most, max=most).astype(kind)


def setup_inputs(seed: int = 0) -> dict:
    key_list = jax.random.split(jax.random.key(seed), 16)
    return {
        "inputs": normal_values(key_list[0], (STEPS, ROWS_TOT, D), 1.0, 6.0, ((1, 8),)),
        "w_xz": normal_values(key_list[1], (D, HEADS, 2 * HEAD_DIM), D ** -0.5, 0.0625, ((0, 16), (1, 8))),
        "w_dt": normal_values(key_list[2], (D, HEADS), D ** -0.5, 0.0625, ((0, 16), (1, 8))),
        "w_bc": normal_values(key_list[3], (D, BC_WIDTH), D ** -0.5, 0.0625, ((0, 16), (1, 8))),
        "w_out": normal_values(key_list[4], (HEADS, HEAD_DIM, D), INNER ** -0.5, 0.0625, ((0, 8), (2, 16))),
        "head_map": jax.random.permutation(key_list[5], SLICES).astype(jnp.int32),
        "a_log": jnp.clip(jax.random.uniform(key_list[6], (HEADS,), jnp.float32, 0.0, 2.77), 0.0, 2.77),
        "dt_bias": jnp.clip(jax.random.uniform(key_list[7], (HEADS,), jnp.float32, -4.0, -1.0), -4.0, -1.0),
        "skip_coef": jnp.clip(jax.random.uniform(key_list[8], (HEADS,), jnp.float32, 0.5, 2.5), 0.5, 2.5),
        "conv_x": normal_values(key_list[9], (KERNEL + 1, INNER), 0.5, 3.0, (), jnp.float32),
        "conv_bc": normal_values(key_list[10], (KERNEL + 1, BC_WIDTH), 0.5, 3.0, (), jnp.float32),
        "norm_gain": jnp.clip(1.0 + 0.15 * jax.random.normal(key_list[11], (INNER,), jnp.float32), 0.25, 1.75),
        "ssm_state": draw_ssm_state(jax.random.fold_in(key_list[15], 71), 0),
        "conv_x_state": normal_values(key_list[13], (ROWS_TOT, KERNEL - 1, INNER), 1.0, 6.0, ((0, 8), (2, 16)), jnp.float32),
        "conv_bc_state": normal_values(key_list[14], (ROWS_TOT, KERNEL - 1, BC_WIDTH), 1.0, 6.0, ((0, 8),), jnp.float32),
    }


EPSILON = 1e-05
HIGHEST = lax.Precision.HIGHEST

def conv_apply(history, fresh_in, conv_taps):
    window = jnp.concatenate([history, fresh_in[:, None, :]], axis=1)
    summed = lax.optimization_barrier(jnp.sum(window * conv_taps[None, :-1, :], axis=1)) + conv_taps[None, -1, :]
    return (jax.nn.silu(summed), window[:, 1:, :])

def reference(inputs, w_xz, w_dt, w_bc, w_out, head_map, a_log, dt_bias, skip_coef, conv_x, conv_bc, norm_gain, ssm_state, conv_x_state, conv_bc_state):
    slot_ids = jnp.arange(HEADS, dtype=jnp.int32)
    slot_head = (head_map[slot_ids // HEAD_SLOTS] + SLICES * (slot_ids % HEAD_SLOTS)).astype(jnp.int32)
    xz_weight = jnp.take(w_xz, slot_head, axis=1).reshape(D, HEADS * 2 * HEAD_DIM)
    dt_weight = jnp.take(w_dt, slot_head, axis=1)
    out_weight = jnp.take(w_out, slot_head, axis=0).reshape(INNER, D)
    a_slot = jnp.take(a_log, slot_head)
    bias_slot = jnp.take(dt_bias, slot_head)
    skip_slot = jnp.take(skip_coef, slot_head)
    gain_slot = jnp.take(norm_gain.reshape(HEADS, HEAD_DIM), slot_head, axis=0)
    taps_x = jnp.take(conv_x.reshape(KERNEL + 1, HEADS, HEAD_DIM), slot_head, axis=1).reshape(KERNEL + 1, INNER)
    group_ids = slot_head // (HEADS // GROUPS)
    onehot = (group_ids[:, None] == jnp.arange(GROUPS, dtype=jnp.int32)[None, :]).astype(jnp.float32)
    group_width = HEADS // GROUPS * HEAD_DIM

    def replica(operands):
        rep_inputs, ssm_now, x_hist, bc_hist = operands
        outputs = []
        for turn_index in range(STEPS):
            x_now = rep_inputs[turn_index]
            proj_xz = jnp.dot(x_now, xz_weight, preferred_element_type=jnp.float32).reshape(ROWS, HEADS, 2 * HEAD_DIM)
            dt_raw = jnp.dot(x_now, dt_weight, preferred_element_type=jnp.float32)
            bc_low = jnp.dot(x_now, w_bc, preferred_element_type=jnp.float32).astype(jnp.bfloat16)
            bc_full = lax.optimization_barrier(bc_low).astype(jnp.float32)
            bc_act, bc_hist = conv_apply(bc_hist, bc_full, conv_bc)
            bc_split = bc_act.reshape(ROWS, GROUPS, 2, STATE)
            b_head = jnp.einsum('tgn,hg->thn', bc_split[:, :, 0], onehot, precision=HIGHEST)
            c_head = jnp.einsum('tgn,hg->thn', bc_split[:, :, 1], onehot, precision=HIGHEST)
            x_act, x_hist = conv_apply(x_hist, proj_xz[:, :, :HEAD_DIM].reshape(ROWS, INNER), taps_x)
            x_act = x_act.reshape(ROWS, HEADS, HEAD_DIM)
            gate_in = proj_xz[:, :, HEAD_DIM:]
            step_size = jax.nn.softplus(dt_raw + bias_slot[None, :])
            decay_rate = jnp.exp(-step_size * jnp.exp(a_slot)[None, :])
            ssm_now = decay_rate[:, :, None, None] * ssm_now + (step_size[:, :, None] * x_act)[:, :, :, None] * b_head[:, :, None, :]
            y_read = jnp.einsum('thpn,thn->thp', ssm_now, c_head, precision=HIGHEST) + skip_slot[None, :, None] * x_act
            gated_out = y_read * jax.nn.silu(gate_in)
            squares = lax.optimization_barrier(jnp.sum(gated_out * gated_out, axis=2))
            group_sums = jnp.dot(squares, onehot, precision=HIGHEST)
            inv_rms = lax.rsqrt(group_sums / group_width + EPSILON)
            per_head = jnp.dot(inv_rms, onehot.T, precision=HIGHEST)
            normed = (gated_out * per_head[:, :, None] * gain_slot[None]).astype(jnp.bfloat16)
            outputs.append(jnp.dot(normed.reshape(ROWS, INNER), out_weight, preferred_element_type=jnp.float32).astype(jnp.bfloat16))
        return (jnp.stack(outputs), ssm_now, x_hist, bc_hist)
    per_replica = (jnp.moveaxis(inputs.reshape(STEPS, N_TP, ROWS, D), 1, 0), ssm_state.reshape(N_TP, ROWS, HEADS, HEAD_DIM, STATE), conv_x_state.reshape(N_TP, ROWS, KERNEL - 1, INNER), conv_bc_state.reshape(N_TP, ROWS, KERNEL - 1, BC_WIDTH))
    mixed, ssm_out, x_out, bc_out = lax.map(replica, per_replica)
    return (jnp.moveaxis(mixed, 0, 1).reshape(STEPS, ROWS_TOT, D), ssm_out.reshape(ROWS_TOT, HEADS, HEAD_DIM, STATE), x_out.reshape(ROWS_TOT, KERNEL - 1, INNER), bc_out.reshape(ROWS_TOT, KERNEL - 1, BC_WIDTH))
```

```python
import jax
import jax.numpy as jnp
from jax import lax
from jax.experimental import pallas as pl
from jax.experimental.pallas import tpu as pltpu
from jax.sharding import PartitionSpec as P

EPSILON = 1e-05
BOTH = ("fsdp", "tp")
F32 = jnp.float32
BF16 = jnp.bfloat16
VMEM_BYTES = 48 * 2**20


def silu(v):
    return v * jax.nn.sigmoid(v)


def project_kernel(map_ref, x_ref, w_ref, wdt_ref, wbc_ref, o_ref, dt_scr, bc_scr):
    part = pl.program_id(0)
    x = x_ref[...]

    @pl.when(part == 0)
    def _():
        bc_scr[...] = jnp.dot(x, wbc_ref[...], preferred_element_type=F32)
        dt_scr[...] = jnp.dot(x, wdt_ref[...], preferred_element_type=F32).T

    per = o_ref.shape[0]
    for k in range(per):
        s = part * per + k
        head = map_ref[s]
        w = w_ref[:, pl.ds(pl.multiple_of(head * 128, 128), 128)]
        y = jnp.dot(x, w, preferred_element_type=F32)
        dt_row = dt_scr[pl.ds(head, 1), :]
        for t in range(8):
            o_ref[k, t, 0:32, :] = y[32 * t : 32 * t + 32, :]
            rows = bc_scr[pl.ds(pl.multiple_of(32 * t + 8 * part, 8), 8), :][2 * k : 2 * k + 2]
            dt = jnp.concatenate(
                [dt_row[:, 32 * t : 32 * t + 32], jnp.zeros((1, 96), F32)], axis=1
            )
            o_ref[k, t, 32:40, :] = jnp.concatenate(
                [rows[:, 0:128], rows[:, 128:256], dt, jnp.zeros((3, 128), F32)], axis=0
            )


def project(head_map, x, w, w_dt, w_bc):
    def whole(*shape):
        return pl.BlockSpec(shape, lambda i, m: (0,) * len(shape))

    return pl.pallas_call(
        project_kernel,
        grid_spec=pltpu.PrefetchScalarGridSpec(
            num_scalar_prefetch=1,
            grid=(4,),
            in_specs=[whole(256, 512), whole(512, 2048), whole(512, 16), whole(512, 256)],
            out_specs=pl.BlockSpec((4, 8, 40, 128), lambda i, m: (i, 0, 0, 0)),
            scratch_shapes=[pltpu.VMEM((16, 256), F32), pltpu.VMEM((256, 256), F32)],
        ),
        out_shape=jax.ShapeDtypeStruct((16, 8, 40, 128), F32),
        compiler_params=pltpu.CompilerParams(vmem_limit_bytes=VMEM_BYTES),
        cost_estimate=pl.CostEstimate(flops=600_000_000, bytes_accessed=5_500_000, transcendentals=0),
        name="project",
    )(head_map, x, w, w_dt, w_bc)


def mixer_kernel(
    coef_ref, par_ref, xz_ref, bc_ref, bc_taps_ref, x_hist_ref, bc_hist_ref, s_ref,
    g_ref, s_out_ref, x_out_ref, bc_out_ref,
):
    group = pl.program_id(0)

    def conv(hist_ref, out_ref, one, two, taps):
        h0, h1, h2 = hist_ref[:, 0, :], hist_ref[:, 1, :], hist_ref[:, 2, :]
        k0, k1, k2, k3, bias = (taps[i : i + 1, :] for i in range(5))
        out_ref[:, 0, :] = h2
        out_ref[:, 1, :] = one
        out_ref[:, 2, :] = two
        first = (h0 * k0 + h1 * k1 + h2 * k2 + one * k3) + bias
        second = (h1 * k0 + h2 * k1 + one * k2 + two * k3) + bias
        return silu(first), silu(second)

    bc = bc_ref[...].astype(F32)
    act1, act2 = conv(bc_hist_ref, bc_out_ref, bc[0:16], bc[16:32], bc_taps_ref[...])
    b1, c1 = act1[:, 0:256], act1[:, 256:512]
    b2, c2 = act2[:, 0:256], act2[:, 256:512]
    lane = lax.broadcasted_iota(jnp.int32, (16, 128), 1)

    def dots(a, b):
        return jnp.sum(a * b, axis=1, keepdims=True)

    pairs = jnp.where(lane == 0, dots(b1, c1), jnp.where(lane == 1, dots(b1, c2), dots(b2, c2))).T
    b1c1, b1c2, b2c2 = pairs[0:1, :], pairs[1:2, :], pairs[2:3, :]

    xz0, xz1 = xz_ref[0, 0:32, :], xz_ref[1, 0:32, :]
    par = par_ref[...]
    x = jnp.concatenate([xz0[:, 0:64], xz1[:, 0:64]], axis=1)
    z = jnp.concatenate([xz0[:, 64:128], xz1[:, 64:128]], axis=1)
    x_act1, x_act2 = conv(x_hist_ref, x_out_ref, x[0:16], x[16:32], par)
    x_act1, x_act2 = x_act1.T, x_act2.T
    gate = silu(z)
    gate1, gate2 = gate[0:16].T, gate[16:32].T
    column = lax.broadcasted_iota(jnp.int32, (64, 16), 1)

    gated = []
    for j in range(2):
        slot = 2 * group + j
        raw = xz_ref[j, 36:37, 0:32] + coef_ref[1, slot]
        step = jnp.maximum(raw, 0.0) + jnp.log1p(jnp.exp(-jnp.abs(raw)))
        rate = jnp.exp(jnp.full((1, 32), coef_ref[0, slot], F32))
        decay = jnp.exp(-step * rate)
        d1, d2 = decay[:, 0:16], decay[:, 16:32]
        half = slice(64 * j, 64 * j + 64)
        xa1, xa2 = x_act1[half], x_act2[half]
        u1, u2 = step[:, 0:16] * xa1, step[:, 16:32] * xa2
        both = d1 * d2
        v1 = d2 * u1
        q1 = jnp.zeros((64, 16), F32)
        q2 = jnp.zeros((64, 16), F32)
        for r in range(16):
            state = s_ref[r, j]
            q1 = jnp.where(column == r, dots(state, c1[r : r + 1, :]), q1)
            q2 = jnp.where(column == r, dots(state, c2[r : r + 1, :]), q2)
            s_out_ref[r, j] = (
                both[:, r : r + 1] * state
                + v1[:, r : r + 1] * b1[r : r + 1, :]
                + u2[:, r : r + 1] * b2[r : r + 1, :]
            )
        y1 = d1 * q1 + u1 * b1c1
        y2 = both * q2 + v1 * b1c2 + u2 * b2c2
        skip = coef_ref[2, slot]
        gated.append(((y1 + skip * xa1) * gate1[half], (y2 + skip * xa2) * gate2[half]))

    sums = [
        sum(jnp.sum(gated[j][i] * gated[j][i], axis=0, keepdims=True) for j in range(2))
        for i in range(2)
    ]
    total = jnp.concatenate(sums + [jnp.zeros((1, 96), F32)], axis=1)
    high = total.astype(BF16).astype(F32)
    tail = jnp.concatenate([high, total - high, jnp.zeros((6, 128), F32)], axis=0)
    for j in range(2):
        gain = par[5:6, 64 * j : 64 * j + 64]
        rows = jnp.concatenate([gated[j][0].T * gain, gated[j][1].T * gain], axis=1)
        g_ref[j] = jnp.concatenate([rows, tail], axis=0).astype(BF16)


def mixer(coef, par, xz, bc, bc_taps, x_hist, bc_hist, state):
    return pl.pallas_call(
        mixer_kernel,
        grid=(4,),
        in_specs=[
            pl.BlockSpec(memory_space=pltpu.SMEM),
            pl.BlockSpec((6, 128), lambda g: (0, g)),
            pl.BlockSpec((2, 40, 128), lambda g: (g, 0, 0)),
            pl.BlockSpec((32, 512), lambda g: (0, g)),
            pl.BlockSpec((5, 512), lambda g: (0, g)),
            pl.BlockSpec((16, 3, 128), lambda g: (0, 0, g)),
            pl.BlockSpec((16, 3, 512), lambda g: (0, 0, g)),
            pl.BlockSpec((16, 2, 64, 256), lambda g: (0, g, 0, 0)),
        ],
        out_specs=(
            pl.BlockSpec((2, 24, 128), lambda g: (g, 0, 0)),
            pl.BlockSpec((16, 2, 64, 256), lambda g: (0, g, 0, 0)),
            pl.BlockSpec((16, 3, 128), lambda g: (0, 0, g)),
            pl.BlockSpec((16, 3, 512), lambda g: (0, 0, g)),
        ),
        out_shape=(
            jax.ShapeDtypeStruct((8, 24, 128), BF16),
            jax.ShapeDtypeStruct(state.shape, F32),
            jax.ShapeDtypeStruct(x_hist.shape, F32),
            jax.ShapeDtypeStruct(bc_hist.shape, F32),
        ),
        compiler_params=pltpu.CompilerParams(vmem_limit_bytes=VMEM_BYTES),
        cost_estimate=pl.CostEstimate(flops=30_000_000, bytes_accessed=17_000_000, transcendentals=100_000),
        name="mixer",
    )(coef, par, xz, bc, bc_taps, x_hist, bc_hist, state)


def output_kernel(map_ref, g_ref, w_ref, o_ref, w_scr, l_scr):
    sums = jnp.zeros((8, 8, 128), F32)
    for s in range(16):
        w_scr[64 * s : 64 * s + 64, :] = w_ref[map_ref[s]]
    for m in range(8):
        even, odd = g_ref[2 * m].astype(F32), g_ref[2 * m + 1].astype(F32)
        sums += even[:, 16:24, :] + odd[:, 16:24, :]
        even = even[:, 0:16, :].reshape(128, 128)
        odd = odd[:, 0:16, :].reshape(128, 128)
        cols = slice(128 * m, 128 * m + 128)
        l_scr[0:128, cols] = jnp.concatenate([even[:, 0:64], odd[:, 0:64]], axis=1).astype(BF16)
        l_scr[128:256, cols] = jnp.concatenate([even[:, 64:], odd[:, 64:]], axis=1).astype(BF16)
    total = sums[:, 0, :] + sums[:, 1, :]
    scale = lax.rsqrt(total / 2048.0 + EPSILON).T
    out = jnp.dot(l_scr[...], w_scr[...], preferred_element_type=F32)
    for t in range(8):
        one = slice(16 * t, 16 * t + 16)
        two = slice(128 + 16 * t, 144 + 16 * t)
        o_ref[t, 0:16, :] = out[one] * scale[0:16, t : t + 1]
        o_ref[t, 16:32, :] = out[two] * scale[16:32, t : t + 1]


def output(head_map, gathered, w_out):
    return pl.pallas_call(
        output_kernel,
        in_specs=[
            pl.BlockSpec(memory_space=pltpu.SMEM),
            pl.BlockSpec(memory_space=pltpu.VMEM),
            pl.BlockSpec(memory_space=pltpu.VMEM),
        ],
        out_specs=pl.BlockSpec(memory_space=pltpu.VMEM),
        out_shape=jax.ShapeDtypeStruct((8, 32, 512), F32),
        scratch_shapes=[pltpu.VMEM((1024, 512), BF16), pltpu.VMEM((256, 1024), BF16)],
        compiler_params=pltpu.CompilerParams(vmem_limit_bytes=VMEM_BYTES),
        cost_estimate=pl.CostEstimate(flops=270_000_000, bytes_accessed=2_500_000, transcendentals=0),
        name="output",
    )(head_map, gathered, w_out)


def per_device(
    inputs, w_xz, w_dt, w_bc, w_out, head_map, a_log, dt_bias, skip_coef,
    conv_x, conv_bc, norm_gain, ssm_state, conv_x_state, conv_bc_state,
):
    me = lax.axis_index("fsdp")
    chosen = head_map[me]
    mine = lax.dynamic_slice_in_dim(inputs.reshape(32, 8192), me * 512, 512, axis=1)
    x = lax.all_to_all(jnp.broadcast_to(mine[None], (8, 32, 512)), "tp", 0, 0, tiled=True)
    partial = project(head_map, x.reshape(256, 512), w_xz.reshape(512, 2048), w_dt, w_bc)
    received = lax.all_to_all(partial.reshape(128, 40, 128), BOTH, 0, 0, tiled=True)
    summed = jnp.sum(received.reshape(16, 8, 40, 128), axis=0)
    low = summed[:, 32:36, :].astype(BF16).reshape(32, 128)
    low = lax.all_to_all(jnp.broadcast_to(low[None], (16, 32, 128)), "fsdp", 0, 0, tiled=True)
    bc = low.reshape(16, 8, 2, 2, 128).transpose(0, 3, 1, 2, 4).reshape(32, 2048)

    table = jnp.concatenate([conv_x, norm_gain[None]], axis=0).reshape(6, 8, 16, 64)
    par = lax.dynamic_index_in_dim(table, chosen, 2, keepdims=False).reshape(6, 512)
    coef = jnp.stack([a_log, dt_bias, skip_coef]).reshape(3, 8, 16)
    coef = lax.dynamic_index_in_dim(coef, chosen, 2, keepdims=False)
    gated, state, x_hist, bc_hist = mixer(
        coef, par, summed, bc, conv_bc, conv_x_state, conv_bc_state, ssm_state
    )
    wide = jnp.broadcast_to(gated[None], (16, 8, 24, 128)).reshape(128, 24, 128)
    gathered = lax.all_to_all(wide, BOTH, 0, 0, tiled=True).reshape(16, 8, 24, 128)
    shares = lax.all_to_all(output(head_map, gathered, w_out), "tp", 0, 0, tiled=True)
    mixed = jnp.sum(shares, axis=0).astype(BF16).reshape(2, 16, 512)
    return mixed, state, x_hist, bc_hist


def solution(mesh):
    return jax.shard_map(
        per_device,
        mesh=mesh,
        in_specs=(
            P(None, "tp", None),
            P("fsdp", "tp", None),
            P("fsdp", "tp"),
            P("fsdp", "tp"),
            P("tp", None, "fsdp"),
            P(), P(), P(), P(), P(), P(), P(),
            P("tp", "fsdp", None, None),
            P("tp", None, "fsdp"),
            P("tp", None, None),
        ),
        out_specs=(
            P(None, "tp", "fsdp"),
            P("tp", "fsdp", None, None),
            P("tp", None, "fsdp"),
            P("tp", None, None),
        ),
        check_vma=False,
    )
```

```python
import functools

import jax
import jax.numpy as jnp
from jax import lax
from jax.experimental import pallas as pl
from jax.experimental.pallas import tpu as pltpu
from jax.sharding import Mesh
from jax.sharding import PartitionSpec as P

EPSILON = 1e-05
F32 = jnp.float32
BF16 = jnp.bfloat16
MIB = 2**20
STATE_MIB = 56
PART = 4


def silu(v):
    return v * jax.nn.sigmoid(v)


def project_kernel(map_ref, pos_ref, x_ref, w_ref, w2_ref, wbd_ref, wbd2_ref, o_ref, dt_scr):
    core = pos_ref[1]
    x1 = x_ref[:, pl.ds(pl.multiple_of(core * 512, 512), 512)]
    x2 = x_ref[:, pl.ds(pl.multiple_of((1 - core) * 512, 512), 512)]

    def dot(w1, w2):
        return jnp.dot(x1, w1, preferred_element_type=F32) + jnp.dot(
            x2, w2, preferred_element_type=F32
        )

    def split(v):
        high = v.astype(BF16).astype(F32)
        return high, v - high

    y = dot(wbd_ref[...], wbd2_ref[...])
    dt_scr[...] = y[:, 256:384].T
    bc_high, bc_low = split(y[:, 0:256])
    none = jnp.zeros((7, 128), F32)
    for i in range(0, 8, 2):
        heads = [map_ref[2 * k + core] for k in (i, i + 1)]
        cols = [pl.ds(pl.multiple_of(head * 128, 128), 128) for head in heads]
        both = dot(
            jnp.concatenate([w_ref[:, c] for c in cols], axis=1),
            jnp.concatenate([w2_ref[:, c] for c in cols], axis=1),
        ).astype(BF16)
        for k in range(2):
            dt_high, dt_low = split(dt_scr[pl.ds(heads[k], 1), :])
            for t in range(8):
                o_ref[i + k, t, 0:32, :] = both[32 * t : 32 * t + 32, 128 * k : 128 * k + 128]
                at = 32 * t + 2 * (i + k)
                high, low = (
                    jnp.concatenate(
                        [
                            jnp.where(core == 0, v[b : b + 1], v[b + 1 : b + 2])
                            for b in (at, at + 16)
                        ],
                        axis=0,
                    )
                    for v in (bc_high, bc_low)
                )
                lanes = slice(32 * t, 32 * t + 32)
                dt = jnp.concatenate([dt_high[:, lanes], dt_low[:, lanes], none[0:1, 0:64]], axis=1)
                o_ref[i + k, t, 32:48, :] = jnp.concatenate(
                    [high[:, 0:128], high[:, 128:256], low[:, 0:128], low[:, 128:256], dt, none],
                    axis=0,
                ).astype(BF16)


HBM = pl.BlockSpec(memory_space=pltpu.HBM)
SMEM = pl.BlockSpec(memory_space=pltpu.SMEM)
VMEM = pl.BlockSpec(memory_space=pltpu.VMEM)


def project(head_map, pos, x, w, w2, wbd, wbd2):
    return pl.pallas_call(
        project_kernel,
        in_specs=[SMEM] * 2 + [VMEM] * 5,
        out_specs=VMEM,
        out_shape=jax.ShapeDtypeStruct((8, 8, 48, 128), BF16),
        scratch_shapes=[pltpu.VMEM((128, 256), F32)],
        compiler_params=pltpu.CompilerParams(vmem_limit_bytes=16 * MIB),
        cost_estimate=pl.CostEstimate(flops=600_000_000, bytes_accessed=5_500_000, transcendentals=0),
        name="project",
    )(head_map, pos, x, w, w2, wbd, wbd2)


def conv(hist_ref, one, two, taps):
    h0, h1, h2 = hist_ref[0], hist_ref[1], hist_ref[2]
    k0, k1, k2, k3, bias = (taps[i : i + 1, :] for i in range(5))
    first = (h0 * k0 + h1 * k1 + h2 * k2 + one * k3) + bias
    second = (h1 * k0 + h2 * k1 + one * k2 + two * k3) + bias
    return silu(first), silu(second)


DECAY, FIRST, SECOND, SKIP, GATE = range(0, 160, 32)


def heads_kernel(
    map_ref, pos_ref, a_ref, bias_ref, skip_ref, taps_ref, gain_ref, xz_ref, x_hist_ref,
    col_ref, x_out_ref, gain_out_ref,
):
    head = map_ref[2 * pos_ref[0] + pos_ref[1]]

    def local(ref):
        parts = []
        for j in range(8):
            block = ref[:, pl.ds(pl.multiple_of(1024 * j + 128 * (head // 2), 128), 128)]
            parts.append(jnp.where(head % 2 == 0, block[:, 0:64], block[:, 64:128]))
        return jnp.concatenate(parts, axis=1)

    def scalars(ref):
        return jnp.concatenate([jnp.full((1, 32), ref[head + 16 * j], F32) for j in range(8)], axis=0)

    gain_out_ref[...] = local(gain_ref)
    rows = [xz_ref[j, 0:32, :] for j in range(8)]
    x = jnp.concatenate([v[:, 0:64] for v in rows], axis=1)
    z = jnp.concatenate([v[:, 64:128] for v in rows], axis=1)
    x_out_ref[0] = x_hist_ref[2]
    x_out_ref[1] = x[0:16]
    x_out_ref[2] = x[16:32]
    x_act = jnp.concatenate(conv(x_hist_ref, x[0:16], x[16:32], local(taps_ref)), axis=0)
    both = jnp.concatenate([x_act, silu(z)], axis=0).T
    raw = jnp.concatenate([xz_ref[j, 40:41, 0:32] + xz_ref[j, 40:41, 32:64] for j in range(8)], axis=0)
    raw = raw + scalars(bias_ref)
    step = jnp.maximum(raw, 0.0) + jnp.log1p(jnp.exp(-jnp.abs(raw)))
    decay = jnp.exp(-step * jnp.exp(scalars(a_ref)))
    ones = jnp.ones((8, 16), F32)
    since = decay * jnp.concatenate([ones, decay[:, 0:16]], axis=1)
    for j in range(8):
        act = both[64 * j : 64 * j + 64, 0:32]
        u = step[j : j + 1, :] * act
        u1, u2 = u[:, 0:16], u[:, 16:32]
        col_ref[j] = jnp.concatenate(
            [
                jnp.broadcast_to(since[j : j + 1, :], (64, 32)),
                u1, decay[j : j + 1, 16:32] * u1,
                jnp.zeros((64, 16), F32), u2,
                skip_ref[head + 16 * j] * act,
                both[64 * j : 64 * j + 64, 32:64],
                jnp.zeros((64, 96), F32),
            ],
            axis=1,
        )


def heads_part(head_map, pos, a_log, dt_bias, skip_coef, conv_x, norm_gain, xz, x_hist):
    return pl.pallas_call(
        heads_kernel,
        in_specs=[SMEM] * 5 + [VMEM] * 4,
        out_specs=(VMEM,) * 3,
        out_shape=(
            jax.ShapeDtypeStruct((8, 64, 256), F32),
            jax.ShapeDtypeStruct(x_hist.shape, F32),
            jax.ShapeDtypeStruct((1, 512), F32),
        ),
        compiler_params=pltpu.CompilerParams(vmem_limit_bytes=16 * MIB),
        cost_estimate=pl.CostEstimate(flops=2_000_000, bytes_accessed=1_000_000, transcendentals=50_000),
        name="heads_part",
    )(head_map, pos, a_log, dt_bias, skip_coef, conv_x, norm_gain[None], xz, x_hist)


def mixer_kernel(
    gain_ref, col_ref, bc_ref, bc_taps_ref, bc_hist_ref, state_ref, g_ref, b_ref, s_ref, sem,
):
    copies = [
        pltpu.make_async_copy(
            state_ref.at[pl.ds(PART * k, PART), pl.ds(2 * g, 2)],
            s_ref.at[g, pl.ds(PART * k, PART)],
            sem.at[g, k],
        )
        for g in range(4)
        for k in range(16 // PART)
    ]
    for copy in copies:
        copy.start()
    bc = jnp.transpose(bc_ref[...].astype(F32), (1, 0, 2))
    one, two = (
        jnp.concatenate([bc[2 * k + step] for k in range(16)], axis=1) for step in range(2)
    )
    act1, act2 = conv(bc_hist_ref, one, two, bc_taps_ref[...])
    lane = lax.broadcasted_iota(jnp.int32, (32, 128), 1)
    column = lax.broadcasted_iota(jnp.int32, (64, 32), 1)

    def dots(a, b):
        return jnp.sum(a * b, axis=1, keepdims=True)

    for g in range(4):
        at = 512 * g
        b1, c1 = act1[:, at : at + 256], act1[:, at + 256 : at + 512]
        b2, c2 = act2[:, at : at + 256], act2[:, at + 256 : at + 512]
        b_ref[g, 0:16, :] = b1
        b_ref[g, 16:32, :] = b2
        with_first = jnp.concatenate([dots(b1, c1), dots(b1, c2)], axis=0)
        with_second = jnp.concatenate([jnp.zeros((16, 1), F32), dots(b2, c2)], axis=0)
        pairs = jnp.where(lane == 0, with_first, with_second).T
        gated = []
        for copy in copies[g * 16 // PART : (g + 1) * 16 // PART]:
            copy.wait()
        for j in (2 * g, 2 * g + 1):
            decay, first, second, skip, gate = (
                col_ref[j, :, k : k + 32] for k in (DECAY, FIRST, SECOND, SKIP, GATE)
            )
            q = jnp.zeros((64, 32), F32)
            for r in range(16):
                state = s_ref[g, r, j - 2 * g]
                q = jnp.where(column == r, dots(state, c1[r : r + 1, :]), q)
                q = jnp.where(column == r + 16, dots(state, c2[r : r + 1, :]), q)
            y = decay * q + first * pairs[0:1, :] + second * pairs[1:2, :]
            gated.append((y + skip) * gate)
        total = sum(jnp.sum(v * v, axis=0, keepdims=True) for v in gated)
        total = jnp.concatenate([total, jnp.zeros((1, 96), F32)], axis=1)
        high = total.astype(BF16).astype(F32)
        tail = jnp.concatenate([high, total - high, jnp.zeros((6, 128), F32)], axis=0)
        rows = jnp.concatenate(gated, axis=0).T * gain_ref[0:1, 128 * g : 128 * g + 128]
        for j in range(2):
            lanes = slice(64 * j, 64 * j + 64)
            block = jnp.concatenate(
                [jnp.concatenate([rows[0:16, lanes], rows[16:32, lanes]], axis=1), tail], axis=0
            ).astype(BF16)
            for chip in range(8):
                g_ref[chip, 2 * g + j] = block


def mixer(gain, cols, bc, bc_taps, bc_hist, state):
    return pl.pallas_call(
        mixer_kernel,
        in_specs=[VMEM] * 5 + [HBM],
        out_specs=(VMEM,) * 2,
        out_shape=(
            jax.ShapeDtypeStruct((8, 8, 24, 128), BF16),
            jax.ShapeDtypeStruct((4, 32, 256), F32),
        ),
        scratch_shapes=[pltpu.VMEM((4, 16, 2, 64, 256), F32), pltpu.SemaphoreType.DMA((4, 16 // PART))],
        compiler_params=pltpu.CompilerParams(vmem_limit_bytes=STATE_MIB * MIB),
        cost_estimate=pl.CostEstimate(flops=20_000_000, bytes_accessed=9_000_000, transcendentals=100_000),
        name="mixer",
    )(gain, cols, bc, bc_taps, bc_hist, state)


def advance_kernel(start, col_ref, b_ref, state_ref, *refs):
    def body(col_ref, b_ref, s_ref, out_ref):
        for j in range(2):
            cols = col_ref[j]
            for r in range(16):
                k = 16 + r
                out_ref[r, j] = (
                    cols[0:1, DECAY + k : DECAY + k + 1] * s_ref[r, j]
                    + cols[:, FIRST + k : FIRST + k + 1] * b_ref[r : r + 1, :]
                    + cols[:, SECOND + k : SECOND + k + 1] * b_ref[k : k + 1, :]
                )

    pltpu.emit_pipeline(
        body,
        grid=(2,),
        in_specs=[
            pl.BlockSpec((2, 64, 256), lambda g: (g + start, 0, 0)),
            pl.BlockSpec((None, 32, 256), lambda g: (g + start, 0, 0)),
            pl.BlockSpec((16, 2, 64, 256), lambda g: (0, g + start, 0, 0)),
        ],
        out_specs=[pl.BlockSpec((16, 2, 64, 256), lambda g: (0, g + start, 0, 0))],
    )(col_ref, b_ref, state_ref, refs[-1])


def advance(cols, b, state, start, into):
    more = [] if into is None else [into]
    return pl.pallas_call(
        functools.partial(advance_kernel, start),
        in_specs=[pl.BlockSpec(memory_space=pl.ANY)] * 2 + [HBM] * (1 + len(more)),
        out_specs=HBM,
        out_shape=jax.ShapeDtypeStruct(state.shape, F32),
        input_output_aliases={3: 0} if more else {},
        compiler_params=pltpu.CompilerParams(vmem_limit_bytes=STATE_MIB * MIB),
        cost_estimate=pl.CostEstimate(flops=6_000_000, bytes_accessed=8_500_000, transcendentals=0),
        name="advance",
    )(cols, b, state, *more)


def output_kernel(map_ref, pos_ref, g1_ref, g2_ref, w_ref, o_ref, w_scr, l_scr):
    sums = jnp.zeros((8, 8, 128), F32)
    core = pos_ref[1]
    for s in range(16):
        which = core if s % 2 == 0 else 1 - core
        w_scr[64 * s : 64 * s + 64, :] = w_ref[map_ref[s // 2 * 2 + which]]
    for m in range(8):
        even, odd = g1_ref[m].astype(F32), g2_ref[m].astype(F32)
        sums += even[:, 16:24, :] + odd[:, 16:24, :]
        even = even[:, 0:16, :].reshape(128, 128)
        odd = odd[:, 0:16, :].reshape(128, 128)
        cols = slice(128 * m, 128 * m + 128)
        l_scr[0:128, cols] = jnp.concatenate([even[:, 0:64], odd[:, 0:64]], axis=1).astype(BF16)
        l_scr[128:256, cols] = jnp.concatenate([even[:, 64:], odd[:, 64:]], axis=1).astype(BF16)
    total = sums[:, 0, :] + sums[:, 1, :]
    scale = lax.rsqrt(total / 2048.0 + EPSILON).T
    out = jnp.dot(l_scr[...], w_scr[...], preferred_element_type=F32)
    for t in range(8):
        one = slice(16 * t, 16 * t + 16)
        two = slice(128 + 16 * t, 144 + 16 * t)
        o_ref[t, 0:16, :] = (out[one] * scale[0:16, t : t + 1]).astype(BF16)
        o_ref[t, 16:32, :] = (out[two] * scale[16:32, t : t + 1]).astype(BF16)


def output(head_map, pos, gathered, other, w_out):
    return pl.pallas_call(
        output_kernel,
        in_specs=[SMEM] * 2 + [VMEM] * 3,
        out_specs=VMEM,
        out_shape=jax.ShapeDtypeStruct((8, 32, 512), BF16),
        scratch_shapes=[pltpu.VMEM((1024, 512), BF16), pltpu.VMEM((256, 1024), BF16)],
        compiler_params=pltpu.CompilerParams(vmem_limit_bytes=16 * MIB),
        cost_estimate=pl.CostEstimate(flops=270_000_000, bytes_accessed=2_500_000, transcendentals=0),
        name="output",
    )(head_map, pos, gathered, other, w_out)


def per_device(
    inputs, w_xz, w_dt, w_bc, w_out, head_map, a_log, dt_bias, skip_coef,
    conv_x, conv_bc, norm_gain, ssm_state, conv_x_state, conv_bc_state,
):
    chip, core = lax.axis_index("chip"), lax.axis_index("core")
    pos = jnp.stack([chip, core]).astype(jnp.int32)

    def swap(v):
        return lax.ppermute(v, "core", [(0, 1), (1, 0)])

    w = w_xz.reshape(512, 2048)
    wbd = jnp.concatenate([w_bc, w_dt, jnp.zeros((512, 112), BF16)], axis=1)
    w2, wbd2 = swap(w_xz).reshape(512, 2048), swap(wbd)
    x = lax.dynamic_slice_in_dim(inputs.reshape(32, 8192), chip * 1024, 1024, axis=1)
    x = lax.all_to_all(jnp.broadcast_to(x[None], (8, 32, 1024)), "tp", 0, 0, tiled=True)
    partial = project(head_map, pos, x.reshape(256, 1024), w, w2, wbd, wbd2)
    received = lax.all_to_all(partial.reshape(64, 48, 128), ("chip", "tp"), 0, 0, tiled=True)
    summed = jnp.sum(received.reshape(8, 8, 48, 128).astype(F32), axis=0)
    cols, x_hist, gain = heads_part(
        head_map, pos, a_log, dt_bias, skip_coef, conv_x, norm_gain, summed,
        conv_x_state.transpose(1, 0, 2),
    )
    low = (summed[:, 32:36, :] + summed[:, 36:40, :]).astype(BF16).reshape(32, 128)
    low = lax.all_to_all(
        jnp.broadcast_to(low[None], (16, 32, 128)), ("chip", "core"), 0, 0, tiled=True
    )

    gated, b = mixer(gain, cols, low, conv_bc, conv_bc_state.transpose(1, 0, 2), ssm_state)
    gathered = lax.all_to_all(gated.reshape(64, 24, 128), ("chip", "tp"), 0, 0, tiled=True).reshape(8, 8, 24, 128)
    fresh = low.reshape(16, 8, 2, 2, 128).transpose(3, 0, 1, 2, 4).reshape(2, 16, 2048)
    bc_hist = jnp.concatenate([conv_bc_state.transpose(1, 0, 2)[2:], fresh.astype(F32)], axis=0)
    state = advance(cols, b, ssm_state, 0, None)
    gathered, state = lax.optimization_barrier((gathered, state))
    state = advance(cols, b, ssm_state, 2, state)
    shares = output(head_map, pos, gathered, swap(gathered), w_out)
    shares = lax.all_to_all(shares, "tp", 0, 0, tiled=True)
    mixed = jnp.sum(shares.astype(F32), axis=0).astype(BF16).reshape(2, 16, 512)
    return mixed, state, x_hist.transpose(1, 0, 2), bc_hist.transpose(1, 0, 2)


def solution(mesh):
    pairs = Mesh(mesh.devices.reshape(8, 2, 8), ("chip", "core", "tp"))
    fsdp = ("chip", "core")
    return jax.shard_map(
        per_device,
        mesh=pairs,
        in_specs=(
            P(None, "tp", None),
            P(fsdp, "tp", None),
            P(fsdp, "tp"),
            P(fsdp, "tp"),
            P("tp", None, fsdp),
            P(), P(), P(), P(), P(), P(), P(),
            P("tp", fsdp, None, None),
            P("tp", None, fsdp),
            P("tp", None, None),
        ),
        out_specs=(
            P(None, "tp", fsdp),
            P("tp", fsdp, None, None),
            P("tp", None, fsdp),
            P("tp", None, None),
        ),
        check_vma=False,
    )
```

```python
import functools

import jax
import jax.numpy as jnp
from jax import lax
from jax.experimental import pallas as pl
from jax.experimental.pallas import tpu as pltpu
from jax.sharding import Mesh
from jax.sharding import PartitionSpec as P

EPSILON = 1e-05
F32 = jnp.float32
BF16 = jnp.bfloat16
MIB = 2**20
STATE_MIB = 50
PART = 4


def silu(v):
    return v * jax.nn.sigmoid(v)


def project_kernel(map_ref, pos_ref, x_ref, w_ref, w2_ref, wbd_ref, wbd2_ref, o_ref, dt_scr):
    core = pos_ref[1]
    x1 = x_ref[:, pl.ds(pl.multiple_of(core * 512, 512), 512)]
    x2 = x_ref[:, pl.ds(pl.multiple_of((1 - core) * 512, 512), 512)]

    def dot(w1, w2):
        return jnp.dot(x1, w1, preferred_element_type=F32) + jnp.dot(
            x2, w2, preferred_element_type=F32
        )

    def split(v):
        high = v.astype(BF16).astype(F32)
        return high, v - high

    y = dot(wbd_ref[...], wbd2_ref[...])
    dt_scr[...] = y[:, 256:384].T
    bc_high, bc_low = split(y[:, 0:256])
    none = jnp.zeros((7, 128), F32)
    for i in range(0, 8, 2):
        heads = [map_ref[2 * k + core] for k in (i, i + 1)]
        cols = [pl.ds(pl.multiple_of(head * 128, 128), 128) for head in heads]
        both = dot(
            jnp.concatenate([w_ref[:, c] for c in cols], axis=1),
            jnp.concatenate([w2_ref[:, c] for c in cols], axis=1),
        ).astype(BF16)
        for k in range(2):
            dt_high, dt_low = split(dt_scr[pl.ds(heads[k], 1), :])
            for t in range(8):
                o_ref[i + k, t, 0:32, :] = both[32 * t : 32 * t + 32, 128 * k : 128 * k + 128]
                at = 32 * t + 2 * (i + k)
                high, low = (
                    jnp.concatenate(
                        [
                            jnp.where(core == 0, v[b : b + 1], v[b + 1 : b + 2])
                            for b in (at, at + 16)
                        ],
                        axis=0,
                    )
                    for v in (bc_high, bc_low)
                )
                lanes = slice(32 * t, 32 * t + 32)
                dt = jnp.concatenate([dt_high[:, lanes], dt_low[:, lanes], none[0:1, 0:64]], axis=1)
                o_ref[i + k, t, 32:48, :] = jnp.concatenate(
                    [high[:, 0:128], high[:, 128:256], low[:, 0:128], low[:, 128:256], dt, none],
                    axis=0,
                ).astype(BF16)


HBM = pl.BlockSpec(memory_space=pltpu.HBM)
SMEM = pl.BlockSpec(memory_space=pltpu.SMEM)
VMEM = pl.BlockSpec(memory_space=pltpu.VMEM)


def project(head_map, pos, x, w, w2, wbd, wbd2):
    return pl.pallas_call(
        project_kernel,
        in_specs=[SMEM] * 2 + [VMEM] * 5,
        out_specs=VMEM,
        out_shape=jax.ShapeDtypeStruct((8, 8, 48, 128), BF16),
        scratch_shapes=[pltpu.VMEM((128, 256), F32)],
        compiler_params=pltpu.CompilerParams(vmem_limit_bytes=16 * MIB),
        cost_estimate=pl.CostEstimate(flops=600_000_000, bytes_accessed=5_500_000, transcendentals=0),
        name="project",
    )(head_map, pos, x, w, w2, wbd, wbd2)


def conv(hist_ref, one, two, taps):
    h0, h1, h2 = hist_ref[0], hist_ref[1], hist_ref[2]
    k0, k1, k2, k3, bias = (taps[i : i + 1, :] for i in range(5))
    first = (h0 * k0 + h1 * k1 + h2 * k2 + one * k3) + bias
    second = (h1 * k0 + h2 * k1 + one * k2 + two * k3) + bias
    return silu(first), silu(second)


DECAY, FIRST, SECOND, SKIP, GATE = range(0, 160, 32)


def heads_kernel(
    map_ref, pos_ref, a_ref, bias_ref, skip_ref, taps_ref, gain_ref, xz_ref, x_hist_ref,
    col_ref, x_out_ref, gain_out_ref,
):
    head = map_ref[2 * pos_ref[0] + pos_ref[1]]

    def local(ref):
        parts = []
        for j in range(8):
            block = ref[:, pl.ds(pl.multiple_of(1024 * j + 128 * (head // 2), 128), 128)]
            parts.append(jnp.where(head % 2 == 0, block[:, 0:64], block[:, 64:128]))
        return jnp.concatenate(parts, axis=1)

    def scalars(ref):
        return jnp.concatenate([jnp.full((1, 32), ref[head + 16 * j], F32) for j in range(8)], axis=0)

    gain_out_ref[...] = local(gain_ref)
    rows = [xz_ref[j, 0:32, :] for j in range(8)]
    x = jnp.concatenate([v[:, 0:64] for v in rows], axis=1)
    z = jnp.concatenate([v[:, 64:128] for v in rows], axis=1)
    x_out_ref[0] = x_hist_ref[2]
    x_out_ref[1] = x[0:16]
    x_out_ref[2] = x[16:32]
    x_act = jnp.concatenate(conv(x_hist_ref, x[0:16], x[16:32], local(taps_ref)), axis=0)
    both = jnp.concatenate([x_act, silu(z)], axis=0).T
    raw = jnp.concatenate([xz_ref[j, 40:41, 0:32] + xz_ref[j, 40:41, 32:64] for j in range(8)], axis=0)
    raw = raw + scalars(bias_ref)
    step = jnp.maximum(raw, 0.0) + jnp.log1p(jnp.exp(-jnp.abs(raw)))
    decay = jnp.exp(-step * jnp.exp(scalars(a_ref)))
    ones = jnp.ones((8, 16), F32)
    since = decay * jnp.concatenate([ones, decay[:, 0:16]], axis=1)
    for j in range(8):
        act = both[64 * j : 64 * j + 64, 0:32]
        u = step[j : j + 1, :] * act
        u1, u2 = u[:, 0:16], u[:, 16:32]
        col_ref[j] = jnp.concatenate(
            [
                jnp.broadcast_to(since[j : j + 1, :], (64, 32)),
                u1, decay[j : j + 1, 16:32] * u1,
                jnp.zeros((64, 16), F32), u2,
                skip_ref[head + 16 * j] * act,
                both[64 * j : 64 * j + 64, 32:64],
                jnp.zeros((64, 96), F32),
            ],
            axis=1,
        )


def heads_part(head_map, pos, a_log, dt_bias, skip_coef, conv_x, norm_gain, xz, x_hist):
    return pl.pallas_call(
        heads_kernel,
        in_specs=[SMEM] * 5 + [VMEM] * 4,
        out_specs=(VMEM,) * 3,
        out_shape=(
            jax.ShapeDtypeStruct((8, 64, 256), F32),
            jax.ShapeDtypeStruct(x_hist.shape, F32),
            jax.ShapeDtypeStruct((1, 512), F32),
        ),
        compiler_params=pltpu.CompilerParams(vmem_limit_bytes=16 * MIB),
        cost_estimate=pl.CostEstimate(flops=2_000_000, bytes_accessed=1_000_000, transcendentals=50_000),
        name="heads_part",
    )(head_map, pos, a_log, dt_bias, skip_coef, conv_x, norm_gain[None], xz, x_hist)


def mixer_kernel(
    gain_ref, col_ref, bc_ref, bc_taps_ref, bc_hist_ref, state_ref, g_ref, b_ref, s_ref, sem,
):
    copies = [
        pltpu.make_async_copy(
            state_ref.at[pl.ds(PART * k, PART), pl.ds(2 * g, 2)],
            s_ref.at[g, pl.ds(PART * k, PART)],
            sem.at[g, k],
        )
        for g in range(4)
        for k in range(16 // PART)
    ]
    for copy in copies:
        copy.start()
    bc = jnp.transpose(bc_ref[...].astype(F32), (1, 0, 2))
    one, two = (
        jnp.concatenate([bc[2 * k + step] for k in range(16)], axis=1) for step in range(2)
    )
    act1, act2 = conv(bc_hist_ref, one, two, bc_taps_ref[...])
    lane = lax.broadcasted_iota(jnp.int32, (32, 128), 1)
    column = lax.broadcasted_iota(jnp.int32, (64, 32), 1)

    def dots(a, b):
        return jnp.sum(a * b, axis=1, keepdims=True)

    for g in range(4):
        at = 512 * g
        b1, c1 = act1[:, at : at + 256], act1[:, at + 256 : at + 512]
        b2, c2 = act2[:, at : at + 256], act2[:, at + 256 : at + 512]
        b_ref[g, 0:16, :] = b1
        b_ref[g, 16:32, :] = b2
        with_first = jnp.concatenate([dots(b1, c1), dots(b1, c2)], axis=0)
        with_second = jnp.concatenate([jnp.zeros((16, 1), F32), dots(b2, c2)], axis=0)
        pairs = jnp.where(lane == 0, with_first, with_second).T
        gated = []
        for copy in copies[g * 16 // PART : (g + 1) * 16 // PART]:
            copy.wait()
        for j in (2 * g, 2 * g + 1):
            decay, first, second, skip, gate = (
                col_ref[j, :, k : k + 32] for k in (DECAY, FIRST, SECOND, SKIP, GATE)
            )
            q = jnp.zeros((64, 32), F32)
            for r in range(16):
                state = s_ref[g, r, j - 2 * g]
                q = jnp.where(column == r, dots(state, c1[r : r + 1, :]), q)
                q = jnp.where(column == r + 16, dots(state, c2[r : r + 1, :]), q)
            y = decay * q + first * pairs[0:1, :] + second * pairs[1:2, :]
            gated.append((y + skip) * gate)
        total = sum(jnp.sum(v * v, axis=0, keepdims=True) for v in gated)
        total = jnp.concatenate([total, jnp.zeros((1, 96), F32)], axis=1)
        high = total.astype(BF16).astype(F32)
        tail = jnp.concatenate([high, total - high, jnp.zeros((6, 128), F32)], axis=0)
        rows = jnp.concatenate(gated, axis=0).T * gain_ref[0:1, 128 * g : 128 * g + 128]
        for j in range(2):
            lanes = slice(64 * j, 64 * j + 64)
            block = jnp.concatenate(
                [jnp.concatenate([rows[0:16, lanes], rows[16:32, lanes]], axis=1), tail], axis=0
            ).astype(BF16)
            for chip in range(8):
                g_ref[chip, 2 * g + j] = block


def mixer(gain, cols, bc, bc_taps, bc_hist, state):
    return pl.pallas_call(
        mixer_kernel,
        in_specs=[VMEM] * 5 + [HBM],
        out_specs=(VMEM,) * 2,
        out_shape=(
            jax.ShapeDtypeStruct((8, 8, 24, 128), BF16),
            jax.ShapeDtypeStruct((4, 32, 256), F32),
        ),
        scratch_shapes=[pltpu.VMEM((4, 16, 2, 64, 256), F32), pltpu.SemaphoreType.DMA((4, 16 // PART))],
        compiler_params=pltpu.CompilerParams(vmem_limit_bytes=STATE_MIB * MIB),
        cost_estimate=pl.CostEstimate(flops=20_000_000, bytes_accessed=9_000_000, transcendentals=100_000),
        name="mixer",
    )(gain, cols, bc, bc_taps, bc_hist, state)


def advance_kernel(start, col_ref, b_ref, state_ref, *refs):
    out_ref, s_ref, n_ref, in_sem, out_sem = refs[-5:]
    chunks = [(g, k) for g in range(2) for k in range(16 // PART)]

    def piece(ref, g, k):
        return ref.at[pl.ds(PART * k, PART), pl.ds(2 * (start + g), 2)]

    def held(ref, g, k):
        return ref.at[g, pl.ds(PART * k, PART)]

    loads = [
        pltpu.make_async_copy(piece(state_ref, g, k), held(s_ref, g, k), in_sem.at[g, k])
        for g, k in chunks
    ]
    stores = [
        pltpu.make_async_copy(held(n_ref, g, k), piece(out_ref, g, k), out_sem.at[g, k])
        for g, k in chunks
    ]
    for load in loads:
        load.start()
    for (g, k), load, store in zip(chunks, loads, stores):
        load.wait()
        for j in range(2):
            cols = col_ref[2 * g + j]
            for r in range(PART * k, PART * k + PART):
                i = 16 + r
                n_ref[g, r, j] = (
                    cols[0:1, DECAY + i : DECAY + i + 1] * s_ref[g, r, j]
                    + cols[:, FIRST + i : FIRST + i + 1] * b_ref[g, r : r + 1, :]
                    + cols[:, SECOND + i : SECOND + i + 1] * b_ref[g, i : i + 1, :]
                )
        store.start()
    for store in stores:
        store.wait()


def advance(cols, b, state, start, into):
    more = [] if into is None else [into]
    return pl.pallas_call(
        functools.partial(advance_kernel, start),
        grid=(1,),
        in_specs=[
            pl.BlockSpec((4, 64, 256), lambda i: (start // 2, 0, 0)),
            pl.BlockSpec((2, 32, 256), lambda i: (start // 2, 0, 0)),
        ] + [HBM] * (1 + len(more)),
        out_specs=HBM,
        out_shape=jax.ShapeDtypeStruct(state.shape, F32),
        scratch_shapes=[
            pltpu.VMEM((2, 16, 2, 64, 256), F32),
            pltpu.VMEM((2, 16, 2, 64, 256), F32),
            pltpu.SemaphoreType.DMA((2, 16 // PART)),
            pltpu.SemaphoreType.DMA((2, 16 // PART)),
        ],
        input_output_aliases={3: 0} if more else {},
        compiler_params=pltpu.CompilerParams(vmem_limit_bytes=STATE_MIB * MIB),
        cost_estimate=pl.CostEstimate(flops=6_000_000, bytes_accessed=8_500_000, transcendentals=0),
        name="advance",
    )(cols, b, state, *more)


def history_kernel(bc_ref, bc_hist_ref, out_ref):
    bc = jnp.transpose(bc_ref[...].astype(F32), (1, 0, 2))
    out_ref[0] = bc_hist_ref[2]
    for step in range(2):
        for k in range(16):
            out_ref[1 + step, :, 128 * k : 128 * k + 128] = bc[2 * k + step]


def history(bc, bc_hist):
    return pl.pallas_call(
        history_kernel,
        in_specs=[VMEM] * 2,
        out_specs=VMEM,
        out_shape=jax.ShapeDtypeStruct(bc_hist.shape, F32),
        compiler_params=pltpu.CompilerParams(vmem_limit_bytes=16 * MIB),
        cost_estimate=pl.CostEstimate(flops=0, bytes_accessed=900_000, transcendentals=0),
        name="history",
    )(bc, bc_hist)


def output_kernel(map_ref, pos_ref, g1_ref, g2_ref, w_ref, o_ref, w_scr, l_scr):
    sums = jnp.zeros((8, 8, 128), F32)
    core = pos_ref[1]
    for s in range(16):
        which = core if s % 2 == 0 else 1 - core
        w_scr[64 * s : 64 * s + 64, :] = w_ref[map_ref[s // 2 * 2 + which]]
    for m in range(8):
        even, odd = g1_ref[m].astype(F32), g2_ref[m].astype(F32)
        sums += even[:, 16:24, :] + odd[:, 16:24, :]
        even = even[:, 0:16, :].reshape(128, 128)
        odd = odd[:, 0:16, :].reshape(128, 128)
        cols = slice(128 * m, 128 * m + 128)
        l_scr[0:128, cols] = jnp.concatenate([even[:, 0:64], odd[:, 0:64]], axis=1).astype(BF16)
        l_scr[128:256, cols] = jnp.concatenate([even[:, 64:], odd[:, 64:]], axis=1).astype(BF16)
    total = sums[:, 0, :] + sums[:, 1, :]
    scale = lax.rsqrt(total / 2048.0 + EPSILON).T
    out = jnp.dot(l_scr[...], w_scr[...], preferred_element_type=F32)
    for t in range(8):
        one = slice(16 * t, 16 * t + 16)
        two = slice(128 + 16 * t, 144 + 16 * t)
        o_ref[t, 0:16, :] = (out[one] * scale[0:16, t : t + 1]).astype(BF16)
        o_ref[t, 16:32, :] = (out[two] * scale[16:32, t : t + 1]).astype(BF16)


def output(head_map, pos, gathered, other, w_out):
    return pl.pallas_call(
        output_kernel,
        in_specs=[SMEM] * 2 + [VMEM] * 3,
        out_specs=VMEM,
        out_shape=jax.ShapeDtypeStruct((8, 32, 512), BF16),
        scratch_shapes=[pltpu.VMEM((1024, 512), BF16), pltpu.VMEM((256, 1024), BF16)],
        compiler_params=pltpu.CompilerParams(vmem_limit_bytes=16 * MIB),
        cost_estimate=pl.CostEstimate(flops=270_000_000, bytes_accessed=2_500_000, transcendentals=0),
        name="output",
    )(head_map, pos, gathered, other, w_out)


def per_device(
    inputs, w_xz, w_dt, w_bc, w_out, head_map, a_log, dt_bias, skip_coef,
    conv_x, conv_bc, norm_gain, ssm_state, conv_x_state, conv_bc_state,
):
    chip, core = lax.axis_index("chip"), lax.axis_index("core")
    pos = jnp.stack([chip, core]).astype(jnp.int32)

    def swap(v):
        return lax.ppermute(v, "core", [(0, 1), (1, 0)])

    w = w_xz.reshape(512, 2048)
    wbd = jnp.concatenate([w_bc, w_dt, jnp.zeros((512, 112), BF16)], axis=1)
    w2, wbd2 = swap(w_xz).reshape(512, 2048), swap(wbd)
    x = lax.dynamic_slice_in_dim(inputs.reshape(32, 8192), chip * 1024, 1024, axis=1)
    x = lax.all_to_all(jnp.broadcast_to(x[None], (8, 32, 1024)), "tp", 0, 0, tiled=True)
    partial = project(head_map, pos, x.reshape(256, 1024), w, w2, wbd, wbd2)
    received = lax.all_to_all(partial.reshape(64, 48, 128), ("chip", "tp"), 0, 0, tiled=True)
    summed = jnp.sum(received.reshape(8, 8, 48, 128).astype(F32), axis=0)
    cols, x_hist, gain = heads_part(
        head_map, pos, a_log, dt_bias, skip_coef, conv_x, norm_gain, summed,
        conv_x_state.transpose(1, 0, 2),
    )
    low = (summed[:, 32:36, :] + summed[:, 36:40, :]).astype(BF16).reshape(32, 128)
    low = lax.all_to_all(
        jnp.broadcast_to(low[None], (16, 32, 128)), ("chip", "core"), 0, 0, tiled=True
    )

    gated, b = mixer(gain, cols, low, conv_bc, conv_bc_state.transpose(1, 0, 2), ssm_state)
    gathered = lax.all_to_all(gated.reshape(64, 24, 128), ("chip", "tp"), 0, 0, tiled=True).reshape(8, 8, 24, 128)
    bc_hist = history(low, conv_bc_state.transpose(1, 0, 2))
    state = advance(cols, b, ssm_state, 0, None)
    gathered, state, bc_hist = lax.optimization_barrier((gathered, state, bc_hist))
    state = advance(cols, b, ssm_state, 2, state)
    shares = output(head_map, pos, gathered, swap(gathered), w_out)
    shares = lax.all_to_all(shares, "tp", 0, 0, tiled=True)
    mixed = jnp.sum(shares.astype(F32), axis=0).astype(BF16).reshape(2, 16, 512)
    return mixed, state, x_hist.transpose(1, 0, 2), bc_hist.transpose(1, 0, 2)


def solution(mesh):
    pairs = Mesh(mesh.devices.reshape(8, 2, 8), ("chip", "core", "tp"))
    fsdp = ("chip", "core")
    return jax.shard_map(
        per_device,
        mesh=pairs,
        in_specs=(
            P(None, "tp", None),
            P(fsdp, "tp", None),
            P(fsdp, "tp"),
            P(fsdp, "tp"),
            P("tp", None, fsdp),
            P(), P(), P(), P(), P(), P(), P(),
            P("tp", fsdp, None, None),
            P("tp", None, fsdp),
            P("tp", None, None),
        ),
        out_specs=(
            P(None, "tp", fsdp),
            P("tp", fsdp, None, None),
            P("tp", None, fsdp),
            P("tp", None, None),
        ),
        check_vma=False,
    )
```

```python
import functools

import jax
import jax.numpy as jnp
from jax import lax
from jax.experimental import pallas as pl
from jax.experimental.pallas import tpu as pltpu
from jax.sharding import Mesh
from jax.sharding import PartitionSpec as P

EPSILON = 1e-05
F32 = jnp.float32
BF16 = jnp.bfloat16
F16 = jnp.float16
SCALE = 128.0
MIB = 2**20
STATE_MIB = 50
PART = 4


def silu(v):
    return v * jax.nn.sigmoid(v)


def project_kernel(map_ref, pos_ref, x_ref, w_ref, w2_ref, wbd_ref, wbd2_ref, o_ref, dt_scr):
    core = pos_ref[1]
    x1 = x_ref[:, pl.ds(pl.multiple_of(core * 512, 512), 512)]
    x2 = x_ref[:, pl.ds(pl.multiple_of((1 - core) * 512, 512), 512)]

    def dot(w1, w2):
        return jnp.dot(x1, w1, preferred_element_type=F32) + jnp.dot(
            x2, w2, preferred_element_type=F32
        )

    y = SCALE * dot(wbd_ref[...], wbd2_ref[...])
    dt_scr[...] = y[:, 256:384].T
    bc = jnp.where(core == 0, y[:, 0:128], y[:, 128:256])
    none = jnp.zeros((8, 96), F32)
    first = lax.broadcasted_iota(jnp.int32, (8, 32), 0) == 0
    for i in range(0, 8, 2):
        heads = [map_ref[2 * k + core] for k in (i, i + 1)]
        cols = [pl.ds(pl.multiple_of(head * 128, 128), 128) for head in heads]
        both = SCALE * dot(
            jnp.concatenate([w_ref[:, c] for c in cols], axis=1),
            jnp.concatenate([w2_ref[:, c] for c in cols], axis=1),
        )
        for k in range(2):
            dt = dt_scr[pl.ds(heads[k], 1), :]
            for t in range(8):
                rows = slice(32 * t, 32 * t + 32)
                o_ref[i + k, t, 0:32, :] = both[rows, 128 * k : 128 * k + 128]
                o_ref[i + k, t, 32:64, :] = bc[rows]
                o_ref[i + k, t, 64:72, :] = jnp.concatenate(
                    [jnp.where(first, dt[:, rows], 0.0), none], axis=1
                )


HBM = pl.BlockSpec(memory_space=pltpu.HBM)
SMEM = pl.BlockSpec(memory_space=pltpu.SMEM)
VMEM = pl.BlockSpec(memory_space=pltpu.VMEM)


def project(head_map, pos, x, w, w2, wbd, wbd2):
    return pl.pallas_call(
        project_kernel,
        in_specs=[SMEM] * 2 + [VMEM] * 5,
        out_specs=VMEM,
        out_shape=jax.ShapeDtypeStruct((8, 8, 72, 128), F32),
        scratch_shapes=[pltpu.VMEM((128, 256), F32)],
        compiler_params=pltpu.CompilerParams(vmem_limit_bytes=16 * MIB),
        cost_estimate=pl.CostEstimate(flops=600_000_000, bytes_accessed=5_500_000, transcendentals=0),
        name="project",
    )(head_map, pos, x, w, w2, wbd, wbd2)


def conv(hist_ref, one, two, taps):
    h0, h1, h2 = hist_ref[0], hist_ref[1], hist_ref[2]
    k0, k1, k2, k3, bias = (taps[i : i + 1, :] for i in range(5))
    first = (h0 * k0 + h1 * k1 + h2 * k2 + one * k3) + bias
    second = (h1 * k0 + h2 * k1 + one * k2 + two * k3) + bias
    return silu(first), silu(second)


DECAY, FIRST, SECOND, SKIP, GATE = range(0, 160, 32)


def heads_kernel(
    map_ref, pos_ref, a_ref, bias_ref, skip_ref, taps_ref, gain_ref, xz_ref, x_hist_ref,
    col_ref, x_out_ref, gain_out_ref,
):
    head = map_ref[2 * pos_ref[0] + pos_ref[1]]

    def local(ref):
        parts = []
        for j in range(8):
            block = ref[:, pl.ds(pl.multiple_of(1024 * j + 128 * (head // 2), 128), 128)]
            parts.append(jnp.where(head % 2 == 0, block[:, 0:64], block[:, 64:128]))
        return jnp.concatenate(parts, axis=1)

    def scalars(ref):
        return jnp.concatenate([jnp.full((1, 32), ref[head + 16 * j], F32) for j in range(8)], axis=0)

    gain_out_ref[...] = local(gain_ref)
    rows = [xz_ref[j, 0:32, :] for j in range(8)]
    x = jnp.concatenate([v[:, 0:64] for v in rows], axis=1)
    z = jnp.concatenate([v[:, 64:128] for v in rows], axis=1)
    x_out_ref[0] = x_hist_ref[2]
    x_out_ref[1] = x[0:16]
    x_out_ref[2] = x[16:32]
    x_act = jnp.concatenate(conv(x_hist_ref, x[0:16], x[16:32], local(taps_ref)), axis=0)
    both = jnp.concatenate([x_act, silu(z)], axis=0).T
    raw = jnp.concatenate([xz_ref[j, 64:65, 0:32] for j in range(8)], axis=0)
    raw = raw + scalars(bias_ref)
    step = jnp.maximum(raw, 0.0) + jnp.log1p(jnp.exp(-jnp.abs(raw)))
    decay = jnp.exp(-step * jnp.exp(scalars(a_ref)))
    ones = jnp.ones((8, 16), F32)
    since = decay * jnp.concatenate([ones, decay[:, 0:16]], axis=1)
    for j in range(8):
        act = both[64 * j : 64 * j + 64, 0:32]
        u = step[j : j + 1, :] * act
        u1, u2 = u[:, 0:16], u[:, 16:32]
        col_ref[j] = jnp.concatenate(
            [
                jnp.broadcast_to(since[j : j + 1, :], (64, 32)),
                u1, decay[j : j + 1, 16:32] * u1,
                jnp.zeros((64, 16), F32), u2,
                skip_ref[head + 16 * j] * act,
                both[64 * j : 64 * j + 64, 32:64],
                jnp.zeros((64, 96), F32),
            ],
            axis=1,
        )


def heads_part(head_map, pos, a_log, dt_bias, skip_coef, conv_x, norm_gain, xz, x_hist):
    return pl.pallas_call(
        heads_kernel,
        in_specs=[SMEM] * 5 + [VMEM] * 4,
        out_specs=(VMEM,) * 3,
        out_shape=(
            jax.ShapeDtypeStruct((8, 64, 256), F32),
            jax.ShapeDtypeStruct(x_hist.shape, F32),
            jax.ShapeDtypeStruct((1, 512), F32),
        ),
        compiler_params=pltpu.CompilerParams(vmem_limit_bytes=16 * MIB),
        cost_estimate=pl.CostEstimate(flops=2_000_000, bytes_accessed=1_000_000, transcendentals=50_000),
        name="heads_part",
    )(head_map, pos, a_log, dt_bias, skip_coef, conv_x, norm_gain[None], xz, x_hist)


def projections(pos_ref, bc_ref, bc2_ref):
    mine, other = bc_ref[...].astype(F32), bc2_ref[...].astype(F32)
    low = jnp.where(pos_ref[1] == 0, mine, other)
    high = jnp.where(pos_ref[1] == 0, other, mine)
    return [
        jnp.concatenate([v[t, 16 * step : 16 * step + 16] for t in range(8) for v in (low, high)], axis=1)
        for step in range(2)
    ]


def mixer_kernel(
    pos_ref, gain_ref, col_ref, bc_ref, bc2_ref, bc_taps_ref, bc_hist_ref, state_ref, g_ref, b_ref, s_ref, sem,
):
    copies = [
        pltpu.make_async_copy(
            state_ref.at[pl.ds(PART * k, PART), pl.ds(2 * g, 2)],
            s_ref.at[g, pl.ds(PART * k, PART)],
            sem.at[g, k],
        )
        for g in range(4)
        for k in range(16 // PART)
    ]
    for copy in copies:
        copy.start()
    one, two = projections(pos_ref, bc_ref, bc2_ref)
    act1, act2 = conv(bc_hist_ref, one, two, bc_taps_ref[...])
    lane = lax.broadcasted_iota(jnp.int32, (32, 128), 1)
    column = lax.broadcasted_iota(jnp.int32, (64, 32), 1)

    def dots(a, b):
        return jnp.sum(a * b, axis=1, keepdims=True)

    for g in range(4):
        at = 512 * g
        b1, c1 = act1[:, at : at + 256], act1[:, at + 256 : at + 512]
        b2, c2 = act2[:, at : at + 256], act2[:, at + 256 : at + 512]
        b_ref[g, 0:16, :] = b1
        b_ref[g, 16:32, :] = b2
        with_first = jnp.concatenate([dots(b1, c1), dots(b1, c2)], axis=0)
        with_second = jnp.concatenate([jnp.zeros((16, 1), F32), dots(b2, c2)], axis=0)
        pairs = jnp.where(lane == 0, with_first, with_second).T
        gated = []
        for copy in copies[g * 16 // PART : (g + 1) * 16 // PART]:
            copy.wait()
        for j in (2 * g, 2 * g + 1):
            decay, first, second, skip, gate = (
                col_ref[j, :, k : k + 32] for k in (DECAY, FIRST, SECOND, SKIP, GATE)
            )
            q = jnp.zeros((64, 32), F32)
            for r in range(16):
                state = s_ref[g, r, j - 2 * g]
                q = jnp.where(column == r, dots(state, c1[r : r + 1, :]), q)
                q = jnp.where(column == r + 16, dots(state, c2[r : r + 1, :]), q)
            y = decay * q + first * pairs[0:1, :] + second * pairs[1:2, :]
            gated.append((y + skip) * gate)
        total = sum(jnp.sum(v * v, axis=0, keepdims=True) for v in gated)
        total = jnp.concatenate([total, jnp.zeros((1, 96), F32)], axis=1)
        high = total.astype(BF16).astype(F32)
        tail = jnp.concatenate([high, total - high, jnp.zeros((6, 128), F32)], axis=0)
        rows = jnp.concatenate(gated, axis=0).T * gain_ref[0:1, 128 * g : 128 * g + 128]
        for j in range(2):
            lanes = slice(64 * j, 64 * j + 64)
            block = jnp.concatenate(
                [jnp.concatenate([rows[0:16, lanes], rows[16:32, lanes]], axis=1), tail], axis=0
            ).astype(BF16)
            for chip in range(8):
                g_ref[chip, 2 * g + j] = block


def mixer(pos, gain, cols, bc, bc2, bc_taps, bc_hist, state):
    return pl.pallas_call(
        mixer_kernel,
        in_specs=[SMEM] + [VMEM] * 6 + [HBM],
        out_specs=(VMEM,) * 2,
        out_shape=(
            jax.ShapeDtypeStruct((8, 8, 24, 128), BF16),
            jax.ShapeDtypeStruct((4, 32, 256), F32),
        ),
        scratch_shapes=[pltpu.VMEM((4, 16, 2, 64, 256), F32), pltpu.SemaphoreType.DMA((4, 16 // PART))],
        compiler_params=pltpu.CompilerParams(vmem_limit_bytes=STATE_MIB * MIB),
        cost_estimate=pl.CostEstimate(flops=20_000_000, bytes_accessed=9_000_000, transcendentals=100_000),
        name="mixer",
    )(pos, gain, cols, bc, bc2, bc_taps, bc_hist, state)


def advance_kernel(start, col_ref, b_ref, state_ref, *refs):
    out_ref, s_ref, n_ref, in_sem, out_sem = refs[-5:]
    chunks = [(g, k) for g in range(2) for k in range(16 // PART)]

    def piece(ref, g, k):
        return ref.at[pl.ds(PART * k, PART), pl.ds(2 * (start + g), 2)]

    def held(ref, g, k):
        return ref.at[g, pl.ds(PART * k, PART)]

    loads = [
        pltpu.make_async_copy(piece(state_ref, g, k), held(s_ref, g, k), in_sem.at[g, k])
        for g, k in chunks
    ]
    stores = [
        pltpu.make_async_copy(held(n_ref, g, k), piece(out_ref, g, k), out_sem.at[g, k])
        for g, k in chunks
    ]
    for load in loads:
        load.start()
    for (g, k), load, store in zip(chunks, loads, stores):
        load.wait()
        for j in range(2):
            cols = col_ref[2 * g + j]
            for r in range(PART * k, PART * k + PART):
                i = 16 + r
                n_ref[g, r, j] = (
                    cols[0:1, DECAY + i : DECAY + i + 1] * s_ref[g, r, j]
                    + cols[:, FIRST + i : FIRST + i + 1] * b_ref[g, r : r + 1, :]
                    + cols[:, SECOND + i : SECOND + i + 1] * b_ref[g, i : i + 1, :]
                )
        store.start()
    for store in stores:
        store.wait()


def advance(cols, b, state, start, into):
    more = [] if into is None else [into]
    return pl.pallas_call(
        functools.partial(advance_kernel, start),
        grid=(1,),
        in_specs=[
            pl.BlockSpec((4, 64, 256), lambda i: (start // 2, 0, 0)),
            pl.BlockSpec((2, 32, 256), lambda i: (start // 2, 0, 0)),
        ] + [HBM] * (1 + len(more)),
        out_specs=HBM,
        out_shape=jax.ShapeDtypeStruct(state.shape, F32),
        scratch_shapes=[
            pltpu.VMEM((2, 16, 2, 64, 256), F32),
            pltpu.VMEM((2, 16, 2, 64, 256), F32),
            pltpu.SemaphoreType.DMA((2, 16 // PART)),
            pltpu.SemaphoreType.DMA((2, 16 // PART)),
        ],
        input_output_aliases={3: 0} if more else {},
        compiler_params=pltpu.CompilerParams(vmem_limit_bytes=STATE_MIB * MIB),
        cost_estimate=pl.CostEstimate(flops=6_000_000, bytes_accessed=8_500_000, transcendentals=0),
        name="advance",
    )(cols, b, state, *more)


def history_kernel(pos_ref, bc_ref, bc2_ref, bc_hist_ref, out_ref):
    out_ref[0] = bc_hist_ref[2]
    out_ref[1], out_ref[2] = projections(pos_ref, bc_ref, bc2_ref)


def history(pos, bc, bc2, bc_hist):
    return pl.pallas_call(
        history_kernel,
        in_specs=[SMEM] + [VMEM] * 3,
        out_specs=VMEM,
        out_shape=jax.ShapeDtypeStruct(bc_hist.shape, F32),
        compiler_params=pltpu.CompilerParams(vmem_limit_bytes=16 * MIB),
        cost_estimate=pl.CostEstimate(flops=0, bytes_accessed=900_000, transcendentals=0),
        name="history",
    )(pos, bc, bc2, bc_hist)


def output_kernel(map_ref, pos_ref, g1_ref, g2_ref, w_ref, o_ref, w_scr, l_scr):
    sums = jnp.zeros((8, 8, 128), F32)
    core = pos_ref[1]
    for s in range(16):
        which = core if s % 2 == 0 else 1 - core
        w_scr[64 * s : 64 * s + 64, :] = w_ref[map_ref[s // 2 * 2 + which]]
    for m in range(8):
        even, odd = g1_ref[m].astype(F32), g2_ref[m].astype(F32)
        sums += even[:, 16:24, :] + odd[:, 16:24, :]
        even = even[:, 0:16, :].reshape(128, 128)
        odd = odd[:, 0:16, :].reshape(128, 128)
        cols = slice(128 * m, 128 * m + 128)
        l_scr[0:128, cols] = jnp.concatenate([even[:, 0:64], odd[:, 0:64]], axis=1).astype(BF16)
        l_scr[128:256, cols] = jnp.concatenate([even[:, 64:], odd[:, 64:]], axis=1).astype(BF16)
    total = sums[:, 0, :] + sums[:, 1, :]
    scale = lax.rsqrt(total / 2048.0 + EPSILON).T
    out = jnp.dot(l_scr[...], w_scr[...], preferred_element_type=F32)
    for t in range(8):
        one = slice(16 * t, 16 * t + 16)
        two = slice(128 + 16 * t, 144 + 16 * t)
        o_ref[t, 0:16, :] = (out[one] * scale[0:16, t : t + 1]).astype(BF16)
        o_ref[t, 16:32, :] = (out[two] * scale[16:32, t : t + 1]).astype(BF16)


def output(head_map, pos, gathered, other, w_out):
    return pl.pallas_call(
        output_kernel,
        in_specs=[SMEM] * 2 + [VMEM] * 3,
        out_specs=VMEM,
        out_shape=jax.ShapeDtypeStruct((8, 32, 512), BF16),
        scratch_shapes=[pltpu.VMEM((1024, 512), BF16), pltpu.VMEM((256, 1024), BF16)],
        compiler_params=pltpu.CompilerParams(vmem_limit_bytes=16 * MIB),
        cost_estimate=pl.CostEstimate(flops=270_000_000, bytes_accessed=2_500_000, transcendentals=0),
        name="output",
    )(head_map, pos, gathered, other, w_out)


def per_device(
    inputs, w_xz, w_dt, w_bc, w_out, head_map, a_log, dt_bias, skip_coef,
    conv_x, conv_bc, norm_gain, ssm_state, conv_x_state, conv_bc_state,
):
    chip, core = lax.axis_index("chip"), lax.axis_index("core")
    pos = jnp.stack([chip, core]).astype(jnp.int32)

    def swap(v):
        return lax.ppermute(v, "core", [(0, 1), (1, 0)])

    w = w_xz.reshape(512, 2048)
    wbd = jnp.concatenate([w_bc, w_dt, jnp.zeros((512, 112), BF16)], axis=1)
    w2, wbd2 = swap(w_xz).reshape(512, 2048), swap(wbd)
    x = lax.dynamic_slice_in_dim(inputs.reshape(32, 8192), chip * 1024, 1024, axis=1)
    x = lax.all_to_all(jnp.broadcast_to(x[None], (8, 32, 1024)), "tp", 0, 0, tiled=True)
    partial = project(head_map, pos, x.reshape(256, 1024), w, w2, wbd, wbd2)
    partial = partial.reshape(64, 72, 128).astype(F16)
    received = lax.all_to_all(partial, ("chip", "tp"), 0, 0, tiled=True)
    summed = jnp.sum(received.reshape(8, 8, 72, 128).astype(F32), axis=0) * (1.0 / SCALE)
    low = summed[:, 32:64, :].astype(BF16)
    low2 = swap(low)
    cols, x_hist, gain = heads_part(
        head_map, pos, a_log, dt_bias, skip_coef, conv_x, norm_gain, summed,
        conv_x_state.transpose(1, 0, 2),
    )
    gated, b = mixer(
        pos, gain, cols, low, low2, conv_bc, conv_bc_state.transpose(1, 0, 2), ssm_state,
    )
    gathered = lax.all_to_all(gated.reshape(64, 24, 128), ("chip", "tp"), 0, 0, tiled=True).reshape(8, 8, 24, 128)
    bc_hist = history(pos, low, low2, conv_bc_state.transpose(1, 0, 2))
    state = advance(cols, b, ssm_state, 0, None)
    gathered, state, bc_hist = lax.optimization_barrier((gathered, state, bc_hist))
    state = advance(cols, b, ssm_state, 2, state)
    shares = output(head_map, pos, gathered, swap(gathered), w_out)
    shares = lax.all_to_all(shares, "tp", 0, 0, tiled=True)
    mixed = jnp.sum(shares.astype(F32), axis=0).astype(BF16).reshape(2, 16, 512)
    return mixed, state, x_hist.transpose(1, 0, 2), bc_hist.transpose(1, 0, 2)


def solution(mesh):
    pairs = Mesh(mesh.devices.reshape(8, 2, 8), ("chip", "core", "tp"))
    fsdp = ("chip", "core")
    return jax.shard_map(
        per_device,
        mesh=pairs,
        in_specs=(
            P(None, "tp", None),
            P(fsdp, "tp", None),
            P(fsdp, "tp"),
            P(fsdp, "tp"),
            P("tp", None, fsdp),
            P(), P(), P(), P(), P(), P(), P(),
            P("tp", fsdp, None, None),
            P("tp", None, fsdp),
            P("tp", None, None),
        ),
        out_specs=(
            P(None, "tp", fsdp),
            P("tp", fsdp, None, None),
            P("tp", None, fsdp),
            P("tp", None, None),
        ),
        check_vma=False,
    )
```

```python
import functools

import jax
import jax.numpy as jnp
from jax import lax
from jax.experimental import pallas as pl
from jax.experimental.pallas import tpu as pltpu
from jax.sharding import Mesh
from jax.sharding import PartitionSpec as P

EPSILON = 1e-05
F32 = jnp.float32
BF16 = jnp.bfloat16
F16 = jnp.float16
SCALE = 128.0
MIB = 2**20
STATE_MIB = 50
PART = 4


def silu(v):
    return v * jax.nn.sigmoid(v)


def project_kernel(map_ref, pos_ref, x_ref, x2_ref, w_ref, w2_ref, wbd_ref, wbd2_ref, o_ref, dt_scr):
    core = pos_ref[1]
    x1, x2 = x_ref[...], x2_ref[...]

    def dot(w1, w2):
        return jnp.dot(x1, w1, preferred_element_type=F32) + jnp.dot(
            x2, w2, preferred_element_type=F32
        )

    y = SCALE * dot(wbd_ref[...], wbd2_ref[...])
    dt_scr[...] = y[:, 256:384].T
    bc = jnp.where(core == 0, y[:, 0:128], y[:, 128:256])
    none = jnp.zeros((8, 96), F32)
    first = lax.broadcasted_iota(jnp.int32, (8, 32), 0) == 0
    for i in range(0, 8, 2):
        heads = [map_ref[2 * k + core] for k in (i, i + 1)]
        cols = [pl.ds(pl.multiple_of(head * 128, 128), 128) for head in heads]
        both = SCALE * dot(
            jnp.concatenate([w_ref[:, c] for c in cols], axis=1),
            jnp.concatenate([w2_ref[:, c] for c in cols], axis=1),
        )
        for k in range(2):
            dt = dt_scr[pl.ds(heads[k], 1), :]
            for t in range(8):
                rows = slice(32 * t, 32 * t + 32)
                o_ref[i + k, t, 0:32, :] = both[rows, 128 * k : 128 * k + 128]
                o_ref[i + k, t, 32:64, :] = bc[rows]
                o_ref[i + k, t, 64:72, :] = jnp.concatenate(
                    [jnp.where(first, dt[:, rows], 0.0), none], axis=1
                )


HBM = pl.BlockSpec(memory_space=pltpu.HBM)
SMEM = pl.BlockSpec(memory_space=pltpu.SMEM)
VMEM = pl.BlockSpec(memory_space=pltpu.VMEM)


def project(head_map, pos, x, x2, w, w2, wbd, wbd2):
    return pl.pallas_call(
        project_kernel,
        in_specs=[SMEM] * 2 + [VMEM] * 6,
        out_specs=VMEM,
        out_shape=jax.ShapeDtypeStruct((8, 8, 72, 128), F32),
        scratch_shapes=[pltpu.VMEM((128, 256), F32)],
        compiler_params=pltpu.CompilerParams(vmem_limit_bytes=16 * MIB),
        cost_estimate=pl.CostEstimate(flops=600_000_000, bytes_accessed=5_500_000, transcendentals=0),
        name="project",
    )(head_map, pos, x, x2, w, w2, wbd, wbd2)


def conv(hist_ref, one, two, taps):
    h0, h1, h2 = hist_ref[0], hist_ref[1], hist_ref[2]
    k0, k1, k2, k3, bias = (taps[i : i + 1, :] for i in range(5))
    first = (h0 * k0 + h1 * k1 + h2 * k2 + one * k3) + bias
    second = (h1 * k0 + h2 * k1 + one * k2 + two * k3) + bias
    return silu(first), silu(second)


DECAY, FIRST, SECOND, SKIP, GATE = range(0, 160, 32)


def heads_kernel(
    map_ref, pos_ref, a_ref, bias_ref, skip_ref, taps_ref, gain_ref, xz_ref, x_hist_ref,
    col_ref, x_out_ref, gain_out_ref,
):
    head = map_ref[2 * pos_ref[0] + pos_ref[1]]

    def local(ref):
        parts = []
        for j in range(8):
            block = ref[:, pl.ds(pl.multiple_of(1024 * j + 128 * (head // 2), 128), 128)]
            parts.append(jnp.where(head % 2 == 0, block[:, 0:64], block[:, 64:128]))
        return jnp.concatenate(parts, axis=1)

    def scalars(ref):
        return jnp.concatenate([jnp.full((1, 32), ref[head + 16 * j], F32) for j in range(8)], axis=0)

    gain_out_ref[...] = local(gain_ref)
    rows = [xz_ref[j, 0:32, :] for j in range(8)]
    x = jnp.concatenate([v[:, 0:64] for v in rows], axis=1)
    z = jnp.concatenate([v[:, 64:128] for v in rows], axis=1)
    x_out_ref[0] = x_hist_ref[2]
    x_out_ref[1] = x[0:16]
    x_out_ref[2] = x[16:32]
    x_act = jnp.concatenate(conv(x_hist_ref, x[0:16], x[16:32], local(taps_ref)), axis=0)
    both = jnp.concatenate([x_act, silu(z)], axis=0).T
    raw = jnp.concatenate([xz_ref[j, 64:65, 0:32] for j in range(8)], axis=0)
    raw = raw + scalars(bias_ref)
    step = jnp.maximum(raw, 0.0) + jnp.log1p(jnp.exp(-jnp.abs(raw)))
    decay = jnp.exp(-step * jnp.exp(scalars(a_ref)))
    ones = jnp.ones((8, 16), F32)
    since = decay * jnp.concatenate([ones, decay[:, 0:16]], axis=1)
    for j in range(8):
        act = both[64 * j : 64 * j + 64, 0:32]
        u = step[j : j + 1, :] * act
        u1, u2 = u[:, 0:16], u[:, 16:32]
        col_ref[j] = jnp.concatenate(
            [
                jnp.broadcast_to(since[j : j + 1, :], (64, 32)),
                u1, decay[j : j + 1, 16:32] * u1,
                jnp.zeros((64, 16), F32), u2,
                skip_ref[head + 16 * j] * act,
                both[64 * j : 64 * j + 64, 32:64],
                jnp.zeros((64, 96), F32),
            ],
            axis=1,
        )


def heads_part(head_map, pos, a_log, dt_bias, skip_coef, conv_x, norm_gain, xz, x_hist):
    return pl.pallas_call(
        heads_kernel,
        in_specs=[SMEM] * 5 + [VMEM] * 4,
        out_specs=(VMEM,) * 3,
        out_shape=(
            jax.ShapeDtypeStruct((8, 64, 256), F32),
            jax.ShapeDtypeStruct(x_hist.shape, F32),
            jax.ShapeDtypeStruct((1, 512), F32),
        ),
        compiler_params=pltpu.CompilerParams(vmem_limit_bytes=16 * MIB),
        cost_estimate=pl.CostEstimate(flops=2_000_000, bytes_accessed=1_000_000, transcendentals=50_000),
        name="heads_part",
    )(head_map, pos, a_log, dt_bias, skip_coef, conv_x, norm_gain[None], xz, x_hist)


def projections(pos_ref, bc_ref, bc2_ref):
    mine, other = bc_ref[...].astype(F32), bc2_ref[...].astype(F32)
    low = jnp.where(pos_ref[1] == 0, mine, other)
    high = jnp.where(pos_ref[1] == 0, other, mine)
    return [
        jnp.concatenate([v[t, 16 * step : 16 * step + 16] for t in range(8) for v in (low, high)], axis=1)
        for step in range(2)
    ]


def mixer_kernel(
    pos_ref, gain_ref, col_ref, bc_ref, bc2_ref, bc_taps_ref, bc_hist_ref, state_ref, g_ref, b_ref, s_ref, sem,
):
    copies = [
        pltpu.make_async_copy(
            state_ref.at[pl.ds(PART * k, PART), pl.ds(2 * g, 2)],
            s_ref.at[g, pl.ds(PART * k, PART)],
            sem.at[g, k],
        )
        for g in range(4)
        for k in range(16 // PART)
    ]
    for copy in copies:
        copy.start()
    one, two = projections(pos_ref, bc_ref, bc2_ref)
    act1, act2 = conv(bc_hist_ref, one, two, bc_taps_ref[...])
    lane = lax.broadcasted_iota(jnp.int32, (32, 128), 1)
    column = lax.broadcasted_iota(jnp.int32, (64, 32), 1)

    def dots(a, b):
        return jnp.sum(a * b, axis=1, keepdims=True)

    for g in range(4):
        at = 512 * g
        b1, c1 = act1[:, at : at + 256], act1[:, at + 256 : at + 512]
        b2, c2 = act2[:, at : at + 256], act2[:, at + 256 : at + 512]
        b_ref[g, 0:16, :] = b1
        b_ref[g, 16:32, :] = b2
        with_first = jnp.concatenate([dots(b1, c1), dots(b1, c2)], axis=0)
        with_second = jnp.concatenate([jnp.zeros((16, 1), F32), dots(b2, c2)], axis=0)
        pairs = jnp.where(lane == 0, with_first, with_second).T
        gated = []
        for copy in copies[g * 16 // PART : (g + 1) * 16 // PART]:
            copy.wait()
        for j in (2 * g, 2 * g + 1):
            decay, first, second, skip, gate = (
                col_ref[j, :, k : k + 32] for k in (DECAY, FIRST, SECOND, SKIP, GATE)
            )
            q = jnp.zeros((64, 32), F32)
            for r in range(16):
                state = s_ref[g, r, j - 2 * g]
                q = jnp.where(column == r, dots(state, c1[r : r + 1, :]), q)
                q = jnp.where(column == r + 16, dots(state, c2[r : r + 1, :]), q)
            y = decay * q + first * pairs[0:1, :] + second * pairs[1:2, :]
            gated.append((y + skip) * gate)
        total = sum(jnp.sum(v * v, axis=0, keepdims=True) for v in gated)
        total = jnp.concatenate([total, jnp.zeros((1, 96), F32)], axis=1)
        high = total.astype(BF16).astype(F32)
        tail = jnp.concatenate([high, total - high, jnp.zeros((6, 128), F32)], axis=0)
        rows = jnp.concatenate(gated, axis=0).T * gain_ref[0:1, 128 * g : 128 * g + 128]
        for j in range(2):
            lanes = slice(64 * j, 64 * j + 64)
            block = jnp.concatenate(
                [jnp.concatenate([rows[0:16, lanes], rows[16:32, lanes]], axis=1), tail], axis=0
            ).astype(BF16)
            for chip in range(8):
                g_ref[chip, 2 * g + j] = block


def mixer(pos, gain, cols, bc, bc2, bc_taps, bc_hist, state):
    return pl.pallas_call(
        mixer_kernel,
        in_specs=[SMEM] + [VMEM] * 6 + [HBM],
        out_specs=(VMEM,) * 2,
        out_shape=(
            jax.ShapeDtypeStruct((8, 8, 24, 128), BF16),
            jax.ShapeDtypeStruct((4, 32, 256), F32),
        ),
        scratch_shapes=[pltpu.VMEM((4, 16, 2, 64, 256), F32), pltpu.SemaphoreType.DMA((4, 16 // PART))],
        compiler_params=pltpu.CompilerParams(vmem_limit_bytes=STATE_MIB * MIB),
        cost_estimate=pl.CostEstimate(flops=20_000_000, bytes_accessed=9_000_000, transcendentals=100_000),
        name="mixer",
    )(pos, gain, cols, bc, bc2, bc_taps, bc_hist, state)


def advance_kernel(start, col_ref, b_ref, state_ref, *refs):
    out_ref, s_ref, n_ref, in_sem, out_sem = refs[-5:]
    chunks = [(g, k) for g in range(2) for k in range(16 // PART)]

    def piece(ref, g, k):
        return ref.at[pl.ds(PART * k, PART), pl.ds(2 * (start + g), 2)]

    def held(ref, g, k):
        return ref.at[g, pl.ds(PART * k, PART)]

    loads = [
        pltpu.make_async_copy(piece(state_ref, g, k), held(s_ref, g, k), in_sem.at[g, k])
        for g, k in chunks
    ]
    stores = [
        pltpu.make_async_copy(held(n_ref, g, k), piece(out_ref, g, k), out_sem.at[g, k])
        for g, k in chunks
    ]
    for load in loads:
        load.start()
    for (g, k), load, store in zip(chunks, loads, stores):
        load.wait()
        for j in range(2):
            cols = col_ref[2 * g + j]
            for r in range(PART * k, PART * k + PART):
                i = 16 + r
                n_ref[g, r, j] = (
                    cols[0:1, DECAY + i : DECAY + i + 1] * s_ref[g, r, j]
                    + cols[:, FIRST + i : FIRST + i + 1] * b_ref[g, r : r + 1, :]
                    + cols[:, SECOND + i : SECOND + i + 1] * b_ref[g, i : i + 1, :]
                )
        store.start()
    for store in stores:
        store.wait()


def advance(cols, b, state, start, into):
    more = [] if into is None else [into]
    return pl.pallas_call(
        functools.partial(advance_kernel, start),
        grid=(1,),
        in_specs=[
            pl.BlockSpec((4, 64, 256), lambda i: (start // 2, 0, 0)),
            pl.BlockSpec((2, 32, 256), lambda i: (start // 2, 0, 0)),
        ] + [HBM] * (1 + len(more)),
        out_specs=HBM,
        out_shape=jax.ShapeDtypeStruct(state.shape, F32),
        scratch_shapes=[
            pltpu.VMEM((2, 16, 2, 64, 256), F32),
            pltpu.VMEM((2, 16, 2, 64, 256), F32),
            pltpu.SemaphoreType.DMA((2, 16 // PART)),
            pltpu.SemaphoreType.DMA((2, 16 // PART)),
        ],
        input_output_aliases={3: 0} if more else {},
        compiler_params=pltpu.CompilerParams(vmem_limit_bytes=STATE_MIB * MIB),
        cost_estimate=pl.CostEstimate(flops=6_000_000, bytes_accessed=8_500_000, transcendentals=0),
        name="advance",
    )(cols, b, state, *more)


def history_kernel(pos_ref, bc_ref, bc2_ref, bc_hist_ref, out_ref):
    out_ref[0] = bc_hist_ref[2]
    out_ref[1], out_ref[2] = projections(pos_ref, bc_ref, bc2_ref)


def history(pos, bc, bc2, bc_hist):
    return pl.pallas_call(
        history_kernel,
        in_specs=[SMEM] + [VMEM] * 3,
        out_specs=VMEM,
        out_shape=jax.ShapeDtypeStruct(bc_hist.shape, F32),
        compiler_params=pltpu.CompilerParams(vmem_limit_bytes=16 * MIB),
        cost_estimate=pl.CostEstimate(flops=0, bytes_accessed=900_000, transcendentals=0),
        name="history",
    )(pos, bc, bc2, bc_hist)


def share_kernel(mine, map_ref, pos_ref, g_ref, w_ref, *refs):
    w_scr, l_scr = refs[-2:]
    which = pos_ref[1] if mine else 1 - pos_ref[1]
    sums = jnp.zeros((8, 8, 128), F32)
    for s in range(8):
        w_scr[64 * s : 64 * s + 64, :] = w_ref[map_ref[2 * s + which]]
    for m in range(4):
        even, odd = g_ref[2 * m].astype(F32), g_ref[2 * m + 1].astype(F32)
        sums += even[:, 16:24, :] + odd[:, 16:24, :]
        even = even[:, 0:16, :].reshape(128, 128)
        odd = odd[:, 0:16, :].reshape(128, 128)
        cols = slice(128 * m, 128 * m + 128)
        l_scr[0:128, cols] = jnp.concatenate([even[:, 0:64], odd[:, 0:64]], axis=1).astype(BF16)
        l_scr[128:256, cols] = jnp.concatenate([even[:, 64:], odd[:, 64:]], axis=1).astype(BF16)
    out = jnp.dot(l_scr[...], w_scr[...], preferred_element_type=F32)
    if mine:
        out_ref, sums_ref = refs[:2]
        out_ref[...] = out
        sums_ref[...] = sums
        return
    out1_ref, sums1_ref, o_ref = refs[:3]
    out += out1_ref[...]
    sums += sums1_ref[...]
    total = sums[:, 0, :] + sums[:, 1, :]
    scale = lax.rsqrt(total / 2048.0 + EPSILON).T
    for t in range(8):
        one = slice(16 * t, 16 * t + 16)
        two = slice(128 + 16 * t, 144 + 16 * t)
        o_ref[t, 0:16, :] = (out[one] * scale[0:16, t : t + 1]).astype(BF16)
        o_ref[t, 16:32, :] = (out[two] * scale[16:32, t : t + 1]).astype(BF16)


def share(mine, head_map, pos, gathered, w_out, *first):
    if mine:
        shapes = (jax.ShapeDtypeStruct((256, 512), F32), jax.ShapeDtypeStruct((8, 8, 128), F32))
    else:
        shapes = jax.ShapeDtypeStruct((8, 32, 512), BF16)
    return pl.pallas_call(
        functools.partial(share_kernel, mine),
        in_specs=[SMEM] * 2 + [VMEM] * (2 + len(first)),
        out_specs=(VMEM, VMEM) if mine else VMEM,
        out_shape=shapes,
        scratch_shapes=[pltpu.VMEM((512, 512), BF16), pltpu.VMEM((256, 512), BF16)],
        compiler_params=pltpu.CompilerParams(vmem_limit_bytes=16 * MIB),
        cost_estimate=pl.CostEstimate(flops=140_000_000, bytes_accessed=1_500_000, transcendentals=0),
        name="share",
    )(head_map, pos, gathered, w_out, *first)


def per_device(
    inputs, w_xz, w_dt, w_bc, w_out, head_map, a_log, dt_bias, skip_coef,
    conv_x, conv_bc, norm_gain, ssm_state, conv_x_state, conv_bc_state,
):
    chip, core = lax.axis_index("chip"), lax.axis_index("core")
    pos = jnp.stack([chip, core]).astype(jnp.int32)

    def swap(v):
        return lax.ppermute(v, "core", [(0, 1), (1, 0)])

    w = w_xz.reshape(512, 2048)
    wbd = jnp.concatenate([w_bc, w_dt, jnp.zeros((512, 112), BF16)], axis=1)
    w2, wbd2 = swap(w_xz).reshape(512, 2048), swap(wbd)
    x = lax.dynamic_slice_in_dim(inputs.reshape(32, 8192), chip * 1024 + core * 512, 512, axis=1)
    x = lax.all_to_all(jnp.broadcast_to(x[None], (8, 32, 512)), "tp", 0, 0, tiled=True)
    x, w = lax.optimization_barrier((x.reshape(256, 512), w))
    partial = project(head_map, pos, x, swap(x), w, w2, wbd, wbd2)
    partial = partial.reshape(64, 72, 128).astype(F16)
    received = lax.all_to_all(partial, ("chip", "tp"), 0, 0, tiled=True)
    summed = jnp.sum(received.reshape(8, 8, 72, 128).astype(F32), axis=0) * (1.0 / SCALE)
    low = summed[:, 32:64, :].astype(BF16)
    low2 = swap(low)
    cols, x_hist, gain = heads_part(
        head_map, pos, a_log, dt_bias, skip_coef, conv_x, norm_gain, summed,
        conv_x_state.transpose(1, 0, 2),
    )
    gated, b = mixer(
        pos, gain, cols, low, low2, conv_bc, conv_bc_state.transpose(1, 0, 2), ssm_state,
    )
    gathered = lax.all_to_all(gated.reshape(64, 24, 128), ("chip", "tp"), 0, 0, tiled=True).reshape(8, 8, 24, 128)
    bc_hist = history(pos, low, low2, conv_bc_state.transpose(1, 0, 2))
    state = advance(cols, b, ssm_state, 0, None)
    gathered, state, bc_hist = lax.optimization_barrier((gathered, state, bc_hist))
    state = advance(cols, b, ssm_state, 2, state)
    other = swap(gathered)
    first = share(True, head_map, pos, gathered, w_out)
    shares = share(False, head_map, pos, other, w_out, *first)
    shares = lax.all_to_all(shares, "tp", 0, 0, tiled=True)
    mixed = jnp.sum(shares.astype(F32), axis=0).astype(BF16).reshape(2, 16, 512)
    return mixed, state, x_hist.transpose(1, 0, 2), bc_hist.transpose(1, 0, 2)


def solution(mesh):
    pairs = Mesh(mesh.devices.reshape(8, 2, 8), ("chip", "core", "tp"))
    fsdp = ("chip", "core")
    return jax.shard_map(
        per_device,
        mesh=pairs,
        in_specs=(
            P(None, "tp", None),
            P(fsdp, "tp", None),
            P(fsdp, "tp"),
            P(fsdp, "tp"),
            P("tp", None, fsdp),
            P(), P(), P(), P(), P(), P(), P(),
            P("tp", fsdp, None, None),
            P("tp", None, fsdp),
            P("tp", None, None),
        ),
        out_specs=(
            P(None, "tp", fsdp),
            P("tp", fsdp, None, None),
            P("tp", None, fsdp),
            P("tp", None, None),
        ),
        check_vma=False,
    )
```

```python
import functools

import jax
import jax.numpy as jnp
from jax import lax
from jax.experimental import pallas as pl
from jax.experimental.pallas import tpu as pltpu
from jax.sharding import Mesh
from jax.sharding import PartitionSpec as P

EPSILON = 1e-05
F32 = jnp.float32
BF16 = jnp.bfloat16
F16 = jnp.float16
SCALE = 128.0
MIB = 2**20
STATE_MIB = 50
PART = 4


def silu(v):
    return v * jax.nn.sigmoid(v)


def project_kernel(map_ref, pos_ref, x_ref, x2_ref, w_ref, w2_ref, wbd_ref, wbd2_ref, o_ref, dt_scr):
    core = pos_ref[1]
    x1, x2 = x_ref[...], x2_ref[...]

    def dot(w1, w2):
        return jnp.dot(x1, w1, preferred_element_type=F32) + jnp.dot(
            x2, w2, preferred_element_type=F32
        )

    y = SCALE * dot(wbd_ref[...], wbd2_ref[...])
    dt_scr[...] = y[:, 256:384].T
    bc = jnp.where(core == 0, y[:, 0:128], y[:, 128:256])
    none = jnp.zeros((8, 96), F32)
    first = lax.broadcasted_iota(jnp.int32, (8, 32), 0) == 0
    for i in range(0, 8, 2):
        heads = [map_ref[2 * k + core] for k in (i, i + 1)]
        cols = [pl.ds(pl.multiple_of(head * 128, 128), 128) for head in heads]
        both = SCALE * dot(
            jnp.concatenate([w_ref[:, c] for c in cols], axis=1),
            jnp.concatenate([w2_ref[:, c] for c in cols], axis=1),
        )
        for k in range(2):
            dt = dt_scr[pl.ds(heads[k], 1), :]
            for t in range(8):
                rows = slice(32 * t, 32 * t + 32)
                o_ref[i + k, t, 0:32, :] = both[rows, 128 * k : 128 * k + 128]
                o_ref[i + k, t, 32:64, :] = bc[rows]
                o_ref[i + k, t, 64:72, :] = jnp.concatenate(
                    [jnp.where(first, dt[:, rows], 0.0), none], axis=1
                )


HBM = pl.BlockSpec(memory_space=pltpu.HBM)
SMEM = pl.BlockSpec(memory_space=pltpu.SMEM)
VMEM = pl.BlockSpec(memory_space=pltpu.VMEM)


def project(head_map, pos, x, x2, w, w2, wbd, wbd2):
    return pl.pallas_call(
        project_kernel,
        in_specs=[SMEM] * 2 + [VMEM] * 6,
        out_specs=VMEM,
        out_shape=jax.ShapeDtypeStruct((8, 8, 72, 128), F32),
        scratch_shapes=[pltpu.VMEM((128, 256), F32)],
        compiler_params=pltpu.CompilerParams(vmem_limit_bytes=16 * MIB),
        cost_estimate=pl.CostEstimate(flops=600_000_000, bytes_accessed=5_500_000, transcendentals=0),
        name="project",
    )(head_map, pos, x, x2, w, w2, wbd, wbd2)


def conv(hist_ref, one, two, taps):
    h0, h1, h2 = hist_ref[0], hist_ref[1], hist_ref[2]
    k0, k1, k2, k3, bias = (taps[i : i + 1, :] for i in range(5))
    first = (h0 * k0 + h1 * k1 + h2 * k2 + one * k3) + bias
    second = (h1 * k0 + h2 * k1 + one * k2 + two * k3) + bias
    return silu(first), silu(second)


DECAY, FIRST, SECOND, SKIP, GATE = range(0, 160, 32)


def heads_part(
    map_ref, pos_ref, a_ref, bias_ref, skip_ref, taps_ref, gain_ref, xz_ref, x_hist_ref,
    col_ref, x_out_ref,
):
    head = map_ref[2 * pos_ref[0] + pos_ref[1]]

    def local(ref):
        parts = []
        for j in range(8):
            block = ref[:, pl.ds(pl.multiple_of(1024 * j + 128 * (head // 2), 128), 128)]
            parts.append(jnp.where(head % 2 == 0, block[:, 0:64], block[:, 64:128]))
        return jnp.concatenate(parts, axis=1)

    def scalars(ref):
        return jnp.concatenate([jnp.full((1, 32), ref[head + 16 * j], F32) for j in range(8)], axis=0)

    rows = [xz_ref[j, 0:32, :] for j in range(8)]
    x = jnp.concatenate([v[:, 0:64] for v in rows], axis=1)
    z = jnp.concatenate([v[:, 64:128] for v in rows], axis=1)
    x_out_ref[0] = x_hist_ref[2]
    x_out_ref[1] = x[0:16]
    x_out_ref[2] = x[16:32]
    x_act = jnp.concatenate(conv(x_hist_ref, x[0:16], x[16:32], local(taps_ref)), axis=0)
    both = jnp.concatenate([x_act, silu(z)], axis=0).T
    raw = jnp.concatenate([xz_ref[j, 64:65, 0:32] for j in range(8)], axis=0)
    raw = raw + scalars(bias_ref)
    step = jnp.maximum(raw, 0.0) + jnp.log1p(jnp.exp(-jnp.abs(raw)))
    decay = jnp.exp(-step * jnp.exp(scalars(a_ref)))
    ones = jnp.ones((8, 16), F32)
    since = decay * jnp.concatenate([ones, decay[:, 0:16]], axis=1)
    for j in range(8):
        act = both[64 * j : 64 * j + 64, 0:32]
        u = step[j : j + 1, :] * act
        u1, u2 = u[:, 0:16], u[:, 16:32]
        col_ref[j] = jnp.concatenate(
            [
                jnp.broadcast_to(since[j : j + 1, :], (64, 32)),
                u1, decay[j : j + 1, 16:32] * u1,
                jnp.zeros((64, 16), F32), u2,
                skip_ref[head + 16 * j] * act,
                both[64 * j : 64 * j + 64, 32:64],
                jnp.zeros((64, 96), F32),
            ],
            axis=1,
        )
    return local(gain_ref)


def projections(pos_ref, bc_ref, bc2_ref):
    mine, other = bc_ref[...].astype(F32), bc2_ref[...].astype(F32)
    low = jnp.where(pos_ref[1] == 0, mine, other)
    high = jnp.where(pos_ref[1] == 0, other, mine)
    return [
        jnp.concatenate([v[t, 16 * step : 16 * step + 16] for t in range(8) for v in (low, high)], axis=1)
        for step in range(2)
    ]


def mixer_kernel(
    map_ref, pos_ref, a_ref, bias_ref, skip_ref, taps_ref, gain_ref, xz_ref, x_hist_ref,
    bc_ref, bc2_ref, bc_taps_ref, bc_hist_ref, state_ref,
    g_ref, b_ref, col_ref, x_out_ref, s_ref, sem,
):
    copies = [
        pltpu.make_async_copy(
            state_ref.at[pl.ds(PART * k, PART), pl.ds(2 * g, 2)],
            s_ref.at[g, pl.ds(PART * k, PART)],
            sem.at[g, k],
        )
        for g in range(4)
        for k in range(16 // PART)
    ]
    for copy in copies:
        copy.start()
    gain = heads_part(
        map_ref, pos_ref, a_ref, bias_ref, skip_ref, taps_ref, gain_ref, xz_ref, x_hist_ref,
        col_ref, x_out_ref,
    )
    one, two = projections(pos_ref, bc_ref, bc2_ref)
    act1, act2 = conv(bc_hist_ref, one, two, bc_taps_ref[...])
    lane = lax.broadcasted_iota(jnp.int32, (32, 128), 1)
    column = lax.broadcasted_iota(jnp.int32, (64, 32), 1)

    def dots(a, b):
        return jnp.sum(a * b, axis=1, keepdims=True)

    for g in range(4):
        at = 512 * g
        b1, c1 = act1[:, at : at + 256], act1[:, at + 256 : at + 512]
        b2, c2 = act2[:, at : at + 256], act2[:, at + 256 : at + 512]
        b_ref[g, 0:16, :] = b1
        b_ref[g, 16:32, :] = b2
        with_first = jnp.concatenate([dots(b1, c1), dots(b1, c2)], axis=0)
        with_second = jnp.concatenate([jnp.zeros((16, 1), F32), dots(b2, c2)], axis=0)
        pairs = jnp.where(lane == 0, with_first, with_second).T
        gated = []
        for copy in copies[g * 16 // PART : (g + 1) * 16 // PART]:
            copy.wait()
        for j in (2 * g, 2 * g + 1):
            decay, first, second, skip, gate = (
                col_ref[j, :, k : k + 32] for k in (DECAY, FIRST, SECOND, SKIP, GATE)
            )
            q = jnp.zeros((64, 32), F32)
            for r in range(16):
                state = s_ref[g, r, j - 2 * g]
                q = jnp.where(column == r, dots(state, c1[r : r + 1, :]), q)
                q = jnp.where(column == r + 16, dots(state, c2[r : r + 1, :]), q)
            y = decay * q + first * pairs[0:1, :] + second * pairs[1:2, :]
            gated.append((y + skip) * gate)
        total = sum(jnp.sum(v * v, axis=0, keepdims=True) for v in gated)
        total = jnp.concatenate([total, jnp.zeros((1, 96), F32)], axis=1)
        high = total.astype(BF16).astype(F32)
        tail = jnp.concatenate([high, total - high, jnp.zeros((6, 128), F32)], axis=0)
        rows = jnp.concatenate(gated, axis=0).T * gain[:, 128 * g : 128 * g + 128]
        for j in range(2):
            lanes = slice(64 * j, 64 * j + 64)
            block = jnp.concatenate(
                [jnp.concatenate([rows[0:16, lanes], rows[16:32, lanes]], axis=1), tail], axis=0
            ).astype(BF16)
            for chip in range(8):
                g_ref[chip, 2 * g + j] = block


def mixer(
    head_map, pos, a_log, dt_bias, skip_coef, conv_x, norm_gain, xz, x_hist,
    bc, bc2, bc_taps, bc_hist, state,
):
    return pl.pallas_call(
        mixer_kernel,
        in_specs=[SMEM] * 5 + [VMEM] * 8 + [HBM],
        out_specs=(VMEM,) * 4,
        out_shape=(
            jax.ShapeDtypeStruct((8, 8, 24, 128), BF16),
            jax.ShapeDtypeStruct((4, 32, 256), F32),
            jax.ShapeDtypeStruct((8, 64, 256), F32),
            jax.ShapeDtypeStruct(x_hist.shape, F32),
        ),
        scratch_shapes=[pltpu.VMEM((4, 16, 2, 64, 256), F32), pltpu.SemaphoreType.DMA((4, 16 // PART))],
        compiler_params=pltpu.CompilerParams(vmem_limit_bytes=STATE_MIB * MIB),
        cost_estimate=pl.CostEstimate(flops=20_000_000, bytes_accessed=9_000_000, transcendentals=100_000),
        name="mixer",
    )(
        head_map, pos, a_log, dt_bias, skip_coef, conv_x, norm_gain[None], xz, x_hist,
        bc, bc2, bc_taps, bc_hist, state,
    )


def advance_kernel(start, col_ref, b_ref, state_ref, *refs):
    out_ref, s_ref, n_ref, in_sem, out_sem = refs[-5:]
    chunks = [(g, k) for g in range(2) for k in range(16 // PART)]

    def piece(ref, g, k):
        return ref.at[pl.ds(PART * k, PART), pl.ds(2 * (start + g), 2)]

    def held(ref, g, k):
        return ref.at[g, pl.ds(PART * k, PART)]

    loads = [
        pltpu.make_async_copy(piece(state_ref, g, k), held(s_ref, g, k), in_sem.at[g, k])
        for g, k in chunks
    ]
    stores = [
        pltpu.make_async_copy(held(n_ref, g, k), piece(out_ref, g, k), out_sem.at[g, k])
        for g, k in chunks
    ]
    for load in loads:
        load.start()
    for (g, k), load, store in zip(chunks, loads, stores):
        load.wait()
        for j in range(2):
            cols = col_ref[2 * g + j]
            for r in range(PART * k, PART * k + PART):
                i = 16 + r
                n_ref[g, r, j] = (
                    cols[0:1, DECAY + i : DECAY + i + 1] * s_ref[g, r, j]
                    + cols[:, FIRST + i : FIRST + i + 1] * b_ref[g, r : r + 1, :]
                    + cols[:, SECOND + i : SECOND + i + 1] * b_ref[g, i : i + 1, :]
                )
        store.start()
    for store in stores:
        store.wait()


def advance(cols, b, state, start, into):
    more = [] if into is None else [into]
    return pl.pallas_call(
        functools.partial(advance_kernel, start),
        grid=(1,),
        in_specs=[
            pl.BlockSpec((4, 64, 256), lambda i: (start // 2, 0, 0)),
            pl.BlockSpec((2, 32, 256), lambda i: (start // 2, 0, 0)),
        ] + [HBM] * (1 + len(more)),
        out_specs=HBM,
        out_shape=jax.ShapeDtypeStruct(state.shape, F32),
        scratch_shapes=[
            pltpu.VMEM((2, 16, 2, 64, 256), F32),
            pltpu.VMEM((2, 16, 2, 64, 256), F32),
            pltpu.SemaphoreType.DMA((2, 16 // PART)),
            pltpu.SemaphoreType.DMA((2, 16 // PART)),
        ],
        input_output_aliases={3: 0} if more else {},
        compiler_params=pltpu.CompilerParams(vmem_limit_bytes=STATE_MIB * MIB),
        cost_estimate=pl.CostEstimate(flops=6_000_000, bytes_accessed=8_500_000, transcendentals=0),
        name="advance",
    )(cols, b, state, *more)


def history_kernel(pos_ref, bc_ref, bc2_ref, bc_hist_ref, out_ref):
    out_ref[0] = bc_hist_ref[2]
    out_ref[1], out_ref[2] = projections(pos_ref, bc_ref, bc2_ref)


def history(pos, bc, bc2, bc_hist):
    return pl.pallas_call(
        history_kernel,
        in_specs=[SMEM] + [VMEM] * 3,
        out_specs=VMEM,
        out_shape=jax.ShapeDtypeStruct(bc_hist.shape, F32),
        compiler_params=pltpu.CompilerParams(vmem_limit_bytes=16 * MIB),
        cost_estimate=pl.CostEstimate(flops=0, bytes_accessed=900_000, transcendentals=0),
        name="history",
    )(pos, bc, bc2, bc_hist)


def share_kernel(mine, map_ref, pos_ref, g_ref, w_ref, *refs):
    w_scr, l_scr = refs[-2:]
    which = pos_ref[1] if mine else 1 - pos_ref[1]
    sums = jnp.zeros((8, 8, 128), F32)
    for s in range(8):
        w_scr[64 * s : 64 * s + 64, :] = w_ref[map_ref[2 * s + which]]
    for m in range(4):
        even, odd = g_ref[2 * m].astype(F32), g_ref[2 * m + 1].astype(F32)
        sums += even[:, 16:24, :] + odd[:, 16:24, :]
        even = even[:, 0:16, :].reshape(128, 128)
        odd = odd[:, 0:16, :].reshape(128, 128)
        cols = slice(128 * m, 128 * m + 128)
        l_scr[0:128, cols] = jnp.concatenate([even[:, 0:64], odd[:, 0:64]], axis=1).astype(BF16)
        l_scr[128:256, cols] = jnp.concatenate([even[:, 64:], odd[:, 64:]], axis=1).astype(BF16)
    out = jnp.dot(l_scr[...], w_scr[...], preferred_element_type=F32)
    if mine:
        out_ref, sums_ref = refs[:2]
        out_ref[...] = out
        sums_ref[...] = sums
        return
    out1_ref, sums1_ref, o_ref = refs[:3]
    out += out1_ref[...]
    sums += sums1_ref[...]
    total = sums[:, 0, :] + sums[:, 1, :]
    scale = lax.rsqrt(total / 2048.0 + EPSILON).T
    for t in range(8):
        one = slice(16 * t, 16 * t + 16)
        two = slice(128 + 16 * t, 144 + 16 * t)
        o_ref[t, 0:16, :] = (out[one] * scale[0:16, t : t + 1]).astype(BF16)
        o_ref[t, 16:32, :] = (out[two] * scale[16:32, t : t + 1]).astype(BF16)


def share(mine, head_map, pos, gathered, w_out, *first):
    if mine:
        shapes = (jax.ShapeDtypeStruct((256, 512), F32), jax.ShapeDtypeStruct((8, 8, 128), F32))
    else:
        shapes = jax.ShapeDtypeStruct((8, 32, 512), BF16)
    return pl.pallas_call(
        functools.partial(share_kernel, mine),
        in_specs=[SMEM] * 2 + [VMEM] * (2 + len(first)),
        out_specs=(VMEM, VMEM) if mine else VMEM,
        out_shape=shapes,
        scratch_shapes=[pltpu.VMEM((512, 512), BF16), pltpu.VMEM((256, 512), BF16)],
        compiler_params=pltpu.CompilerParams(vmem_limit_bytes=16 * MIB),
        cost_estimate=pl.CostEstimate(flops=140_000_000, bytes_accessed=1_500_000, transcendentals=0),
        name="share",
    )(head_map, pos, gathered, w_out, *first)


def per_device(
    inputs, w_xz, w_dt, w_bc, w_out, head_map, a_log, dt_bias, skip_coef,
    conv_x, conv_bc, norm_gain, ssm_state, conv_x_state, conv_bc_state,
):
    chip, core = lax.axis_index("chip"), lax.axis_index("core")
    pos = jnp.stack([chip, core]).astype(jnp.int32)

    def swap(v):
        return lax.ppermute(v, "core", [(0, 1), (1, 0)])

    w = w_xz.reshape(512, 2048)
    wbd = jnp.concatenate([w_bc, w_dt, jnp.zeros((512, 112), BF16)], axis=1)
    w2, wbd2 = swap(w_xz).reshape(512, 2048), swap(wbd)
    x = lax.dynamic_slice_in_dim(inputs.reshape(32, 8192), chip * 1024 + core * 512, 512, axis=1)
    x = lax.all_to_all(jnp.broadcast_to(x[None], (8, 32, 512)), "tp", 0, 0, tiled=True)
    x, w = lax.optimization_barrier((x.reshape(256, 512), w))
    partial = project(head_map, pos, x, swap(x), w, w2, wbd, wbd2)
    partial = partial.reshape(64, 72, 128).astype(F16)
    received = lax.all_to_all(partial, ("chip", "tp"), 0, 0, tiled=True)
    summed = jnp.sum(received.reshape(8, 8, 72, 128).astype(F32), axis=0) * (1.0 / SCALE)
    low = summed[:, 32:64, :].astype(BF16)
    low2 = swap(low)
    gated, b, cols, x_hist = mixer(
        head_map, pos, a_log, dt_bias, skip_coef, conv_x, norm_gain, summed,
        conv_x_state.transpose(1, 0, 2), low, low2, conv_bc, conv_bc_state.transpose(1, 0, 2),
        ssm_state,
    )
    gathered = lax.all_to_all(gated.reshape(64, 24, 128), ("chip", "tp"), 0, 0, tiled=True).reshape(8, 8, 24, 128)
    bc_hist = history(pos, low, low2, conv_bc_state.transpose(1, 0, 2))
    state = advance(cols, b, ssm_state, 0, None)
    gathered, state, bc_hist = lax.optimization_barrier((gathered, state, bc_hist))
    state = advance(cols, b, ssm_state, 2, state)
    other = swap(gathered)
    first = share(True, head_map, pos, gathered, w_out)
    shares = share(False, head_map, pos, other, w_out, *first)
    shares = lax.all_to_all(shares, "tp", 0, 0, tiled=True)
    mixed = jnp.sum(shares.astype(F32), axis=0).astype(BF16).reshape(2, 16, 512)
    return mixed, state, x_hist.transpose(1, 0, 2), bc_hist.transpose(1, 0, 2)


def solution(mesh):
    pairs = Mesh(mesh.devices.reshape(8, 2, 8), ("chip", "core", "tp"))
    fsdp = ("chip", "core")
    return jax.shard_map(
        per_device,
        mesh=pairs,
        in_specs=(
            P(None, "tp", None),
            P(fsdp, "tp", None),
            P(fsdp, "tp"),
            P(fsdp, "tp"),
            P("tp", None, fsdp),
            P(), P(), P(), P(), P(), P(), P(),
            P("tp", fsdp, None, None),
            P("tp", None, fsdp),
            P("tp", None, None),
        ),
        out_specs=(
            P(None, "tp", fsdp),
            P("tp", fsdp, None, None),
            P("tp", None, fsdp),
            P("tp", None, None),
        ),
        check_vma=False,
    )
```
